512 devices in a mesh: tile: 128 (over y, x, z_hi, core), sub: 4 (over z_lo).
Axes of the slice: x: 4, y: 8, z: 8 (z_hi: 2, z_lo: 4; z = z_hi * 4 + z_lo), core: 2. Of those that a mesh axis runs over, the one named last changes fastest.
Arguments:
- features: bfloat16 [128, 128, 4096], P('tile', None, 'sub')
- cotangent: bfloat16 [128, 128, 4096], P('tile', None, 'sub')
- conv_weight: bfloat16 [128, 9, 128], replicated, may hold values from -0.1875 to 0.1875
- norm_gain: float32 [128], replicated, may hold values from 0.1 to 1.9
- norm_shift: float32 [128], replicated, may hold values from -3 to 3
- seam_code: int32 [128, 4], P('tile'), may hold values from 0 to 7, as said below
- corner_map: int32 [128, 4], P('tile'), may hold values from 0 to 1, as said below
Outputs:
- grad_input: bfloat16 [128, 128, 4096], P('tile', None, 'sub')
- grad_weight: float32 [128, 9, 128], replicated
- grad_gain: float32 [128], replicated
- grad_shift: float32 [128], replicated
The draws below stay inside these ranges and needn't reach their ends.
Inputs may be any that keep to these rules, and one draw needn't show every extreme that they name: seam_code[t, e] = D + 4 * f: side e faces grid direction D (0: tile t - 4, 1: tile t + 1, 2: tile t + 4, 3: tile t - 1, modulo 128); f = 1 marks a strip that runs reversed across the seam. The four sides of a tile face four different directions. `corner_map`: 0 fills a corner from the side along row 0 or row 65, 1 from the side along column 0 or column 65.
All inputs are finite; a program needn't handle non-finite values.
Results may differ from the reference program's by a relative error of at most 0.002.
The reference program's roundings to bfloat16 on the way count: a program that leaves them out, or rounds other values in their place, can miss the bound.
Values may be sent and summed in bfloat16 or wider, within the bound.
No kernel may reach another device: no remote copies, remote signals or barrier semaphores. Data moves between devices by JAX's collectives and lax.ppermute only.
A program may use at most 64 MiB of HBM per device.

```python
import math
import jax
import jax.numpy as jnp
import numpy as np
from jax import lax

C = 128
GROUPS = 16
GC = 4
S = 64
TILES = 128


def rough_field(key, rise, spread, factor):
    key_a = jax.random.fold_in(key, 0)
    key_c = jax.random.fold_in(key, 2)
    key_d = jax.random.fold_in(key, 3)
    normal_part = jax.random.normal(key_a, (TILES, C, S, S), jnp.float32)
    base_draw = normal_part
    tile_scale = rise ** (jnp.arange(TILES, dtype=jnp.float32) / max(TILES - 1, 1))
    chan_scale = jnp.exp(jax.random.uniform(key_c, (C,), jnp.float32, 0.0, math.log(spread)))
    row_scale = jnp.exp(jax.random.uniform(key_d, (TILES, 1, S, 1), jnp.float32, 0.0, math.log(3.0)))
    values = factor * (base_draw * tile_scale[:, None, None, None] * chan_scale[None, :, None, None] * row_scale)
    return values.reshape(TILES, C, S * S)


def draw_features(key, part):
    key = jax.random.fold_in(key, 21)
    values = rough_field(key, 3.0, 10.0, 0.05)
    return values.astype(jnp.bfloat16)


def draw_cotangent(key, part):
    key = jax.random.fold_in(key, 22)
    values = rough_field(key, 3.0, 3.0, 0.5)
    return values.astype(jnp.bfloat16)


def dihedral_tables():
    normals = np.array([[-1, 0], [0, 1], [1, 0], [0, -1]])
    alongs = np.array([[0, 1], [1, 0], [0, 1], [1, 0]])
    quarter = np.array([[0, 1], [-1, 0]])
    mirror = np.array([[1, 0], [0, -1]])
    matrices = []
    for orient_code in range(8):
        matrix = mirror if orient_code >= 4 else np.eye(2, dtype=np.int64)
        for repeat_index in range(orient_code % 4):
            matrix = quarter @ matrix
        matrices.append(matrix)
    facing = np.zeros((8, 4), np.int32)
    for orient_code in range(8):
        for side_index in range(4):
            normal_out = matrices[orient_code] @ normals[side_index]
            facing[orient_code, side_index] = int(np.argmax((normals == normal_out).all(axis=1)))
    reverse = np.zeros((8, 4, 8), np.int32)
    for orient_code in range(8):
        for side_index in range(4):
            back_dir = (facing[orient_code, side_index] + 2) % 4
            own_along = matrices[orient_code] @ alongs[side_index]
            for other_orient in range(8):
                other_side = int(np.argmax(facing[other_orient] == back_dir))
                theirs = matrices[other_orient] @ alongs[other_side]
                reverse[orient_code, side_index, other_orient] = int((own_along == -theirs).all())
    return (facing, reverse)


def draw_seam_code(key, part):
    key = jax.random.fold_in(key, 11)
    facing_np, reverse_np = dihedral_tables()
    facing = jnp.asarray(facing_np)
    reverse = jnp.asarray(reverse_np)
    tile_ids = jnp.arange(TILES, dtype=jnp.int32)
    face_of = tile_ids * 12 // TILES
    face_turns = jax.random.randint(key, (12,), 0, 8, dtype=jnp.int32)
    orient = face_turns[face_of]
    orient = orient.at[0].set(0).at[1].set(2).at[TILES - GC].set(0)
    step_table = jnp.array([-GC, 1, GC, -1], dtype=jnp.int32)
    direction = facing[orient]
    neighbour = (tile_ids[:, None] + step_table[direction]) % TILES
    reverse_flag = reverse[orient[:, None], jnp.arange(4, dtype=jnp.int32)[None, :], orient[neighbour]]
    return (direction + 4 * reverse_flag).astype(jnp.int32)


def draw_corner_map(key, part):
    key = jax.random.fold_in(key, 12)
    corner_pick = jax.random.randint(key, (TILES, 4), 0, 2, dtype=jnp.int32)
    return corner_pick.at[0, 0].set(0).at[0, 1].set(1)


def normal_values(key, shape, deviation, bound, held_as=jnp.bfloat16):
    values = jax.random.normal(key, shape, jnp.float32) * deviation
    return jnp.minimum(jnp.maximum(values, -bound), bound).astype(held_as)


def setup_inputs(seed: int = 0) -> dict:
    streams_of = jax.random.split(jax.random.key(seed), 8)
    return {
        "features": draw_features(jax.random.fold_in(streams_of[7], 71), 0),
        "cotangent": draw_cotangent(jax.random.fold_in(streams_of[7], 71), 0),
        "conv_weight": normal_values(streams_of[2], (C, 9, C), (9 * C) ** -0.5, 0.1875),
        "norm_gain": jnp.clip(1.0 + 0.18 * jax.random.normal(streams_of[3], (C,), jnp.float32), 0.1, 1.9),
        "norm_shift": normal_values(streams_of[4], (C,), 0.5, 3.0, jnp.float32),
        "seam_code": draw_seam_code(jax.random.fold_in(streams_of[7], 71), 0),
        "corner_map": draw_corner_map(jax.random.fold_in(streams_of[7], 71), 0),
    }


EPSILON = 1e-05

def side_cells(tile_blocks):
    return jnp.stack([tile_blocks[:, :, 0, :], tile_blocks[:, :, :, S - 1], tile_blocks[:, :, S - 1, :], tile_blocks[:, :, :, 0]], axis=1)

def facing_pick(strips, facing, wanted):
    matched = facing == wanted
    return lax.optimization_barrier(jnp.sum(jnp.where(matched[:, :, None, None], strips, jnp.zeros((), strips.dtype)), axis=1))

def reference(features, cotangent, conv_weight, norm_gain, norm_shift, seam_code, corner_map):
    features = features.reshape(TILES, C, S, S)
    cotangent = cotangent.reshape(TILES, C, S, S)
    per_group = C // GROUPS
    entries = per_group * TILES * S * S
    grad_scale = 1.0 / math.sqrt(TILES * S * S)
    offsets = [-GC, 1, GC, -1]
    facing = seam_code % 4
    reversed_flag = seam_code // 4

    def group_sums(tile_block):
        return lax.optimization_barrier(jnp.sum(tile_block.astype(jnp.float32).reshape(GROUPS, per_group * S * S), axis=1))
    group_means = lax.optimization_barrier(jnp.sum(lax.map(group_sums, features), axis=0)) / entries
    mean_c = jnp.repeat(group_means, per_group)[:, None, None]

    def group_spread(tile_block):
        centred = (tile_block.astype(jnp.float32) - mean_c).reshape(GROUPS, per_group * S * S)
        return lax.optimization_barrier(jnp.sum(centred * centred, axis=1))
    spread = lax.optimization_barrier(jnp.sum(lax.map(group_spread, features), axis=0)) / entries
    rstd_c = jnp.repeat(lax.rsqrt(spread + EPSILON), per_group)[:, None, None]
    gain_c = norm_gain[:, None, None]
    shift_c = norm_shift[:, None, None]

    def activate(tile_block):
        normed = (tile_block.astype(jnp.float32) - mean_c) * rstd_c
        return jax.nn.silu(normed * gain_c + shift_c).astype(jnp.bfloat16)
    activation = lax.map(activate, features)
    edge_cells = side_cells(activation)
    arrived = []
    for direction in range(4):
        outgoing = facing_pick(edge_cells, facing, (direction + 2) % 4)
        arrived.append(jnp.roll(outgoing, -offsets[direction], axis=0))
    arrived = jnp.stack(arrived, axis=1)
    match_dir = facing[:, :, None] == jnp.arange(4, dtype=jnp.int32)[None, None, :]
    halo_in = lax.optimization_barrier(jnp.sum(jnp.where(match_dir[:, :, :, None, None], arrived[:, None], jnp.zeros((), arrived.dtype)), axis=2))
    halo_in = jnp.where(reversed_flag[:, :, None, None] == 1, halo_in[..., ::-1], halo_in)
    corners = jnp.stack([jnp.where(corner_map[:, 0:1] == 0, halo_in[:, 0, :, 0], halo_in[:, 3, :, 0]), jnp.where(corner_map[:, 1:2] == 0, halo_in[:, 0, :, S - 1], halo_in[:, 1, :, 0]), jnp.where(corner_map[:, 2:3] == 0, halo_in[:, 2, :, S - 1], halo_in[:, 1, :, S - 1]), jnp.where(corner_map[:, 3:4] == 0, halo_in[:, 2, :, 0], halo_in[:, 3, :, S - 1])], axis=2)

    def tile_backward(inputs):
        act_tile, halo_tile, corner_tile, grad_tile, pick_tile = inputs
        left_line = jnp.concatenate([corner_tile[:, 0:1], halo_tile[3], corner_tile[:, 3:4]], axis=1)
        right_line = jnp.concatenate([corner_tile[:, 1:2], halo_tile[1], corner_tile[:, 2:3]], axis=1)
        middle = jnp.concatenate([halo_tile[0][:, None, :], act_tile, halo_tile[2][:, None, :]], axis=1)
        padded = jnp.concatenate([left_line[:, :, None], middle, right_line[:, :, None]], axis=2)
        grad_flat = grad_tile.reshape(C, S * S)
        weight_parts = []
        pad_grad = jnp.zeros((C, S + 2, S + 2), jnp.float32)
        for tap_index in range(9):
            tap_row = tap_index // 3
            tap_col = tap_index % 3
            window = padded[:, tap_row:tap_row + S, tap_col:tap_col + S].reshape(C, S * S)
            weight_parts.append(lax.dot_general(grad_flat, window, (((1,), (1,)), ((), ())), preferred_element_type=jnp.float32))
            spread_back = jnp.dot(conv_weight[:, tap_index, :].T, grad_flat, preferred_element_type=jnp.float32)
            pad_grad = pad_grad.at[:, tap_row:tap_row + S, tap_col:tap_col + S].add(spread_back.reshape(C, S, S))
        corner_grads = [pad_grad[:, 0, 0], pad_grad[:, 0, S + 1], pad_grad[:, S + 1, S + 1], pad_grad[:, S + 1, 0]]
        top_grad = pad_grad[:, 0, 1:S + 1]
        right_grad = pad_grad[:, 1:S + 1, S + 1]
        bottom_grad = pad_grad[:, S + 1, 1:S + 1]
        left_grad = pad_grad[:, 1:S + 1, 0]

        def chosen(corner_index, wanted):
            return jnp.where(pick_tile[corner_index] == wanted, corner_grads[corner_index], jnp.zeros_like(corner_grads[corner_index]))
        top_grad = top_grad.at[:, 0].add(chosen(0, 0)).at[:, S - 1].add(chosen(1, 0))
        bottom_grad = bottom_grad.at[:, S - 1].add(chosen(2, 0)).at[:, 0].add(chosen(3, 0))
        left_grad = left_grad.at[:, 0].add(chosen(0, 1)).at[:, S - 1].add(chosen(3, 1))
        right_grad = right_grad.at[:, 0].add(chosen(1, 1)).at[:, S - 1].add(chosen(2, 1))
        halo_grad = jnp.stack([top_grad, right_grad, bottom_grad, left_grad], axis=0)
        return (jnp.stack(weight_parts, axis=1), pad_grad[:, 1:S + 1, 1:S + 1], halo_grad.astype(jnp.bfloat16))
    weight_parts, interior, halo_grad = lax.map(tile_backward, (activation, halo_in, corners, cotangent, corner_map))
    weight_total = lax.optimization_barrier(jnp.sum(weight_parts, axis=0))
    turned = jnp.where(reversed_flag[:, :, None, None] == 1, halo_grad[..., ::-1], halo_grad)
    coming = []
    for direction in range(4):
        outgoing = facing_pick(turned, facing, direction)
        coming.append(jnp.roll(outgoing, offsets[direction], axis=0))
    coming = jnp.stack(coming, axis=1)
    back_match = facing[:, :, None] == (jnp.arange(4, dtype=jnp.int32)[None, None, :] + 2) % 4
    returned = lax.optimization_barrier(jnp.sum(jnp.where(back_match[:, :, :, None, None], coming[:, None], jnp.zeros((), coming.dtype)), axis=2)).astype(jnp.float32)
    interior = interior.at[:, :, 0, :].add(returned[:, 0])
    interior = interior.at[:, :, :, S - 1].add(returned[:, 1])
    interior = interior.at[:, :, S - 1, :].add(returned[:, 2])
    interior = interior.at[:, :, :, 0].add(returned[:, 3])

    def pre_grads(tile_block, act_grad):
        normed = (tile_block.astype(jnp.float32) - mean_c) * rstd_c
        pre_act = normed * gain_c + shift_c
        sigmoid_of = jax.nn.sigmoid(pre_act)
        return (normed, act_grad * (sigmoid_of * (1.0 + pre_act * (1.0 - sigmoid_of))))

    def channel_sums(inputs):
        normed, pre_grad = pre_grads(inputs[0], inputs[1])
        return (lax.optimization_barrier(jnp.sum(pre_grad * normed, axis=(1, 2))), lax.optimization_barrier(jnp.sum(pre_grad, axis=(1, 2))))
    gain_parts, shift_parts = lax.map(channel_sums, (features, interior))
    gain_total = lax.optimization_barrier(jnp.sum(gain_parts, axis=0))
    shift_total = lax.optimization_barrier(jnp.sum(shift_parts, axis=0))
    first_mean = (jnp.repeat(lax.optimization_barrier(jnp.sum((norm_gain * shift_total).reshape(GROUPS, per_group), axis=1)), per_group) / entries)[:, None, None]
    second_mean = (jnp.repeat(lax.optimization_barrier(jnp.sum((norm_gain * gain_total).reshape(GROUPS, per_group), axis=1)), per_group) / entries)[:, None, None]

    def input_grad(inputs):
        normed, pre_grad = pre_grads(inputs[0], inputs[1])
        return (rstd_c * (pre_grad * gain_c - first_mean - normed * second_mean)).astype(jnp.bfloat16)
    grad_input = lax.map(input_grad, (features, interior)).reshape(TILES, C, S * S)
    return (grad_input, weight_total * grad_scale, gain_total * grad_scale, shift_total * grad_scale)
```

```python
import math

import jax
import jax.numpy as jnp
from jax import lax
from jax.experimental import pallas as pl
from jax.experimental.pallas import tpu as pltpu
from jax.sharding import Mesh
from jax.sharding import PartitionSpec as P

GC = 4
S = 64
PER_GROUP = 8
EPSILON = 1e-05
STEPS = (-GC, 1, GC, -1)
ROWS = 16
CELLS = ROWS * S
C = 128
EDGE = 2 * S + 2 * ROWS
CHUNK = 24

TILE = ("y", "x", "zh", "co")
AXES = {"y": 8, "x": 4, "zh": 2, "co": 2, "zl": 4}
NEAR = ("zh", "co", "zl")
FAR = ("y", "x")
N_NEAR = 16
N_FAR = 32
DEVICES = 512
ENTRIES = DEVICES * CELLS * PER_GROUP
LOCAL = CELLS * PER_GROUP
SCALE = 1.0 / math.sqrt(DEVICES * CELLS)

F32 = jnp.float32
BF16 = jnp.bfloat16
VMEM = pl.BlockSpec(memory_space=pltpu.VMEM)
SMEM = pl.BlockSpec(memory_space=pltpu.SMEM)
PARAMS = pltpu.CompilerParams(vmem_limit_bytes=40 * 1024 * 1024)


def group_sum(row):
    total = jnp.broadcast_to(row, (8, C))
    lane = lax.broadcasted_iota(jnp.int32, (8, C), 1)
    for by in (1, 2, 4):
        other = jnp.where(
            (lane & by) != 0, pltpu.roll(total, by, 1), pltpu.roll(total, C - by, 1)
        )
        total = total + other
    return total[0:1]


def merge(rows, count):
    means, squares = rows[:, :C], rows[:, C:]
    mean = jnp.sum(means, axis=0, keepdims=True) * (1.0 / rows.shape[0])
    gap = means - mean
    spread = jnp.sum(squares, axis=0, keepdims=True) + float(count) * jnp.sum(
        gap * gap, axis=0, keepdims=True
    )
    return mean, spread


def start_kernel(x_ref, c_ref, xt_ref, ct_ref, edge_ref, stat_ref, x_scr, c_scr):
    x = x_ref[0].astype(F32).T
    x_scr[...] = x
    xt_ref[...] = x.astype(BF16)
    c = c_ref[0].astype(F32).T
    c_scr[...] = c
    ct_ref[...] = c.astype(BF16)
    for base, scr, flat in ((0, x_scr, xt_ref), (EDGE, c_scr, ct_ref)):
        edge_ref[base : base + S] = flat[0:S]
        edge_ref[base + S : base + 2 * S] = flat[CELLS - S : CELLS]
        edge_ref[base + 2 * S : base + 2 * S + ROWS] = scr[
            pl.ds(0, ROWS, stride=S), :
        ].astype(BF16)
        edge_ref[base + 2 * S + ROWS : base + EDGE] = scr[
            pl.ds(S - 1, ROWS, stride=S), :
        ].astype(BF16)
    mean = group_sum(jnp.sum(x, axis=0, keepdims=True)) * (1.0 / LOCAL)
    gap = x - mean
    spread = group_sum(jnp.sum(gap * gap, axis=0, keepdims=True))
    stat_ref[...] = jnp.broadcast_to(
        jnp.concatenate([mean, spread], axis=1), (N_NEAR, 2 * C)
    )


def flip_matrix():
    a = lax.broadcasted_iota(jnp.int32, (S, S), 0)
    b = lax.broadcasted_iota(jnp.int32, (S, S), 1)
    return jnp.where(a + b == S - 1, 1.0, 0.0).astype(BF16)


def turned(strip, flag):
    back = jnp.dot(flip_matrix(), strip, preferred_element_type=F32)
    return jnp.where(flag == 1, back, strip.astype(F32)).astype(BF16)


def seam_kernel(
    place_ref, seam_ref, corner_ref, e0_ref, e1_ref, e2_ref, e3_ref, stat_ref, w_ref,
    m0_ref, m1_ref, m2_ref, m3_ref, rows_ref, out_stat_ref, all_scr, side_scr, grad_scr,
):
    place = place_ref[0]
    for k, ref in enumerate((e0_ref, e1_ref, e2_ref, e3_ref)):
        all_scr[(place + 4 - k) % 4] = ref[...]
    for kind in range(2):
        base = kind * EDGE
        side_scr[kind, 0] = all_scr[0, base : base + S]
        side_scr[kind, 2] = all_scr[3, base + S : base + 2 * S]
        for p in range(4):
            at = slice(p * ROWS, (p + 1) * ROWS)
            side_scr[kind, 3, at] = all_scr[p, base + 2 * S : base + 2 * S + ROWS]
            side_scr[kind, 1, at] = all_scr[p, base + 2 * S + ROWS : base + EDGE]
    row = lax.broadcasted_iota(jnp.int32, (S, C), 0)
    first, last = row == 0, row == S - 1
    taps = ((0, 1, 2), (2, 5, 8), (6, 7, 8), (0, 3, 6))
    ends = (((0, 0), (1, 0)), ((1, 1), (2, 1)), ((3, 0), (2, 0)), ((0, 1), (3, 1)))
    for e in range(4):
        strip = side_scr[1, e]
        parts = [
            jnp.dot(strip, w_ref[:, t * C : (t + 1) * C], preferred_element_type=F32)
            for t in taps[e]
        ]
        (start_at, start_is), (end_at, end_is) = ends[e]
        grad = parts[1]
        grad = grad + jnp.where(last, 0.0, pltpu.roll(parts[0], S - 1, 0))
        grad = grad + jnp.where(first, 0.0, pltpu.roll(parts[2], 1, 0))
        grad = grad + jnp.where(first & (corner_ref[0, start_at] == start_is), parts[0], 0.0)
        grad = grad + jnp.where(last & (corner_ref[0, end_at] == end_is), parts[2], 0.0)
        grad_scr[e] = turned(grad.astype(BF16), seam_ref[0, e] // 4)
    for d, ref in enumerate((m0_ref, m1_ref, m2_ref, m3_ref)):
        side = jnp.int32(0)
        for e in range(1, 4):
            side = jnp.where(seam_ref[0, e] % 4 == d, e, side)
        ref[0:S] = side_scr[0, side]
        ref[S : 2 * S] = grad_scr[side]
    above, below = jnp.maximum(place - 1, 0), jnp.minimum(place + 1, 3)
    rows_ref[0:S] = all_scr[above, S : 2 * S]
    rows_ref[S : 2 * S] = all_scr[below, 0:S]
    zero = jnp.zeros((S, C), BF16)
    rows_ref[2 * S : 3 * S] = jnp.where(place == 0, zero, all_scr[above, EDGE + S : EDGE + 2 * S])
    rows_ref[3 * S : 4 * S] = jnp.where(place == 3, zero, all_scr[below, EDGE : EDGE + S])
    mean, spread = merge(stat_ref[...], LOCAL)
    out_stat_ref[...] = jnp.broadcast_to(
        jnp.concatenate([mean, spread], axis=1), (N_FAR, 2 * C)
    )


def main_kernel(
    place_ref, seam_ref, corner_ref, xt_ref, ct_ref, cot_ref, rows_ref, stat_ref, w_ref,
    gain_ref, shift_ref, a0_ref, a1_ref, a2_ref, a3_ref,
    part_ref, pre_ref, norm_ref, in_scr, line_scr, left_scr, right_scr, act_scr,
):
    place = place_ref[0]
    for d, ref in enumerate((a0_ref, a1_ref, a2_ref, a3_ref)):
        in_scr[(d + 2) % 4] = ref[...]
    mean, spread = merge(stat_ref[...], LOCAL * N_NEAR)
    rstd = lax.rsqrt(spread * (1.0 / ENTRIES) + EPSILON)
    gain, shift = gain_ref[...], shift_ref[...]
    norm_ref[...] = jnp.concatenate([mean, rstd], axis=0)

    def affine(raw):
        normed = (raw.astype(F32) - mean) * rstd
        pre = normed * gain + shift
        return normed, pre, 1.0 / (1.0 + jnp.exp(-pre))

    def activated(raw):
        _, pre, sig = affine(raw)
        return (pre * sig).astype(BF16).astype(F32)

    def strip(e):
        return turned(in_scr[seam_ref[0, e] % 4, 0:S], seam_ref[0, e] // 4)

    top = activated(jnp.where(place == 0, strip(0), rows_ref[0:S]))
    bottom = activated(jnp.where(place == 3, strip(2), rows_ref[S : 2 * S]))
    right, left = activated(strip(1)), activated(strip(3))
    normed, pre, sig = affine(xt_ref[...])
    own = (pre * sig).astype(BF16).astype(F32)
    for k, (line, near, far, a, b, at) in enumerate(
        ((left, 0, 3, 0, 0, 0), (right, 1, 2, S - 1, S - 1, 1))
    ):
        line_scr[k, 8 : 8 + S] = line
        line_scr[k, 7:8] = jnp.where(corner_ref[0, near] == 0, top[a : a + 1], line[0:1])
        line_scr[k, 8 + S : 9 + S] = jnp.where(
            corner_ref[0, far] == 0, bottom[b : b + 1], line[S - 1 : S]
        )
    window = pl.ds(pl.multiple_of(place * ROWS, 8), 32)
    left_part = line_scr[0, window, :][7 : 7 + ROWS + 2]
    right_part = line_scr[1, window, :][7 : 7 + ROWS + 2]
    middle = jnp.concatenate([top, own, bottom], axis=0)
    wide = CELLS + 2 * S
    left_scr[...] = pltpu.roll(middle, 1, 0)
    left_scr[pl.ds(0, ROWS + 2, stride=S), :] = left_part
    right_scr[...] = pltpu.roll(middle, wide - 1, 0)
    right_scr[pl.ds(S - 1, ROWS + 2, stride=S), :] = right_part
    windows = jnp.concatenate(
        [left_scr[...].astype(BF16), middle.astype(BF16), right_scr[...].astype(BF16)], axis=1
    )
    grad_out = cot_ref[0]
    for i in range(3):
        part = jnp.dot(grad_out, windows[i * S : i * S + CELLS], preferred_element_type=F32)
        for j in range(3):
            for h in range(2):
                part_ref[pl.ds(h * 9 + 3 * i + j, 64, stride=CHUNK), :] = part[
                    h * 64 : (h + 1) * 64, j * C : (j + 1) * C
                ]

    grads = jnp.concatenate(
        [rows_ref[2 * S : 3 * S], ct_ref[...], rows_ref[3 * S : 4 * S]], axis=0
    ).astype(F32)
    column = lax.broadcasted_iota(jnp.int32, (wide, C), 0) & (S - 1)
    later = jnp.where(column == S - 1, 0.0, pltpu.roll(grads, wide - 1, 0))
    earlier = jnp.where(column == 0, 0.0, pltpu.roll(grads, 1, 0))
    shifted = jnp.concatenate(
        [later.astype(BF16), grads.astype(BF16), earlier.astype(BF16)], axis=1
    )
    act_grad = None
    for i in range(3):
        weight = jnp.concatenate(
            [w_ref[:, (3 * i + j) * C : (3 * i + j + 1) * C] for j in range(3)], axis=0
        )
        term = jnp.dot(
            shifted[(2 - i) * S : (2 - i) * S + CELLS], weight, preferred_element_type=F32
        )
        act_grad = term if act_grad is None else act_grad + term
    act_scr[...] = act_grad

    def returned(e, start, size):
        at = pl.ds(pl.multiple_of(S + start, 16), size)
        return in_scr[seam_ref[0, e] % 4, at, :].astype(F32)

    own_rows = place * ROWS
    act_scr[pl.ds(0, ROWS, stride=S), :] += returned(3, own_rows, ROWS)
    act_scr[pl.ds(S - 1, ROWS, stride=S), :] += returned(1, own_rows, ROWS)
    act_scr[0:S] += jnp.where(place == 0, returned(0, 0, S), 0.0)
    act_scr[CELLS - S : CELLS] += jnp.where(place == 3, returned(2, 0, S), 0.0)
    pre_grad = act_scr[...] * (sig * (1.0 + pre * (1.0 - sig)))
    pre_ref[...] = pre_grad
    gain_row = jnp.sum(pre_grad * normed, axis=0, keepdims=True)
    shift_row = jnp.sum(pre_grad, axis=0, keepdims=True)
    part_ref[pl.ds(18, 64, stride=CHUNK), :] = jnp.broadcast_to(gain_row, (64, C))
    part_ref[pl.ds(19, 64, stride=CHUNK), :] = jnp.broadcast_to(shift_row, (64, C))
    for k in range(20, CHUNK):
        part_ref[pl.ds(k, 64, stride=CHUNK), :] = jnp.zeros((64, C), F32)


def end_kernel(pre_ref, xt_ref, norm_ref, gain_ref, total_ref, out_ref, sums_ref):
    mean, rstd = norm_ref[0:1], norm_ref[1:2]
    gain = gain_ref[...]
    gain_total, shift_total = total_ref[18:19], total_ref[19:20]
    first = group_sum(gain * shift_total) * (1.0 / ENTRIES)
    second = group_sum(gain * gain_total) * (1.0 / ENTRIES)
    normed = (xt_ref[...].astype(F32) - mean) * rstd
    out = rstd * (pre_ref[...] * gain - first - normed * second)
    out_ref[0] = out.T.astype(BF16)
    sums_ref[...] = jnp.concatenate([gain_total, shift_total], axis=0) * SCALE


def shape(dims, dtype):
    return jax.ShapeDtypeStruct(dims, dtype)


def body(features, cotangent, conv_weight, norm_gain, norm_shift, seam_code, corner_map):
    place = lax.axis_index("zl").astype(jnp.int32).reshape(1)
    weight = conv_weight.reshape(C, 9 * C)
    gain, shift = norm_gain.reshape(1, C), norm_shift.reshape(1, C)
    xt, ct, edges, stats = pl.pallas_call(
        start_kernel,
        out_shape=(
            shape((CELLS, C), BF16),
            shape((CELLS, C), BF16),
            shape((2 * EDGE, C), BF16),
            shape((N_NEAR, 2 * C), F32),
        ),
        in_specs=[VMEM] * 2,
        out_specs=(VMEM,) * 4,
        scratch_shapes=[pltpu.VMEM((CELLS, C), F32)] * 2,
        compiler_params=PARAMS,
    )(features, cotangent)
    others = [
        lax.ppermute(edges, "zl", [(i, (i + by) % 4) for i in range(4)]) for by in (1, 2, 3)
    ]
    stats = lax.all_to_all(stats, NEAR, 0, 0, tiled=True)
    message = shape((2 * S, C), BF16)
    *messages, rows, stats = pl.pallas_call(
        seam_kernel,
        out_shape=(message,) * 4 + (shape((4 * S, C), BF16), shape((N_FAR, 2 * C), F32)),
        in_specs=[SMEM] * 3 + [VMEM] * 6,
        out_specs=(VMEM,) * 6,
        scratch_shapes=[
            pltpu.VMEM((4, 2 * EDGE, C), BF16),
            pltpu.VMEM((2, 4, S, C), BF16),
            pltpu.VMEM((4, S, C), BF16),
        ],
        compiler_params=PARAMS,
    )(place, seam_code, corner_map, edges, *others, stats, weight)
    arrived = [
        lax.ppermute(m, TILE, [(i, (i + by) % 128) for i in range(128)])
        for m, by in zip(messages, STEPS)
    ]
    stats = lax.all_to_all(stats, FAR, 0, 0, tiled=True)
    wide = CELLS + 2 * S
    parts, pre_grad, norm = pl.pallas_call(
        main_kernel,
        out_shape=(shape((64 * CHUNK, C), F32), shape((CELLS, C), F32), shape((2, C), F32)),
        in_specs=[SMEM] * 3 + [VMEM] * 12,
        out_specs=(VMEM,) * 3,
        scratch_shapes=[
            pltpu.VMEM((4, 2 * S, C), BF16),
            pltpu.VMEM((2, 80, C), F32),
            pltpu.VMEM((wide, C), F32),
            pltpu.VMEM((wide, C), F32),
            pltpu.VMEM((CELLS, C), F32),
        ],
        compiler_params=PARAMS,
    )(place, seam_code, corner_map, xt, ct, cotangent, rows, stats, weight, gain, shift, *arrived)
    parts = lax.all_to_all(parts.reshape(2, N_FAR, CHUNK, C), "co", 0, 0, tiled=True)
    parts = lax.all_to_all(jnp.sum(parts, axis=0), FAR, 0, 0, tiled=True)
    part = jnp.sum(parts, axis=0)
    near = lax.all_to_all(
        jnp.broadcast_to(part[None], (8, CHUNK, C)), ("zh", "zl"), 0, 0, tiled=True
    )
    total = jnp.sum(near, axis=0)
    half = lax.all_to_all(
        jnp.broadcast_to(total[None], (N_FAR, CHUNK, C)), FAR, 0, 0, tiled=True
    )
    whole = lax.all_gather(half, "co", axis=0, tiled=True)
    grad_input, sums = pl.pallas_call(
        end_kernel,
        out_shape=(shape((1, C, CELLS), BF16), shape((2, C), F32)),
        in_specs=[VMEM] * 5,
        out_specs=(VMEM,) * 2,
        compiler_params=PARAMS,
    )(pre_grad, xt, norm, gain, total)
    grad_weight = jnp.concatenate([whole[:, 0:9], whole[:, 9:18]], axis=0) * SCALE
    return grad_input, grad_weight, sums[0], sums[1]


def solution(mesh):
    fine = Mesh(mesh.devices.reshape(tuple(AXES.values())), tuple(AXES))
    return jax.shard_map(
        body,
        mesh=fine,
        in_specs=(
            P(TILE, None, "zl"),
            P(TILE, None, "zl"),
            P(),
            P(),
            P(),
            P(TILE, None),
            P(TILE, None),
        ),
        out_specs=(P(TILE, None, "zl"), P(), P(), P()),
        check_vma=False,
    )
```

```python
import functools
import math

import jax
import jax.numpy as jnp
from jax import lax
from jax.experimental import pallas as pl
from jax.experimental.pallas import tpu as pltpu
from jax.sharding import Mesh
from jax.sharding import PartitionSpec as P

GC = 4
S = 64
PER_GROUP = 8
EPSILON = 1e-05
STEPS = (-GC, 1, GC, -1)
ROWS = 16
CELLS = ROWS * S
C = 128
LINE = 2 * S
CHUNK = 20

TILE = ("y", "x", "zh", "co")
AXES = {"y": 8, "x": 4, "zh": 2, "co": 2, "zl": 4}
NEAR = ("zh", "co", "zl")
FAR = ("y", "x")
N_NEAR = 16
N_FAR = 32
DEVICES = 512
ENTRIES = DEVICES * CELLS * PER_GROUP
LOCAL = CELLS * PER_GROUP
SCALE = 1.0 / math.sqrt(DEVICES * CELLS)

F32 = jnp.float32
BF16 = jnp.bfloat16
VMEM = pl.BlockSpec(memory_space=pltpu.VMEM)
SMEM = pl.BlockSpec(memory_space=pltpu.SMEM)
PARAMS = pltpu.CompilerParams(vmem_limit_bytes=40 * 1024 * 1024)


def group_sum(row):
    total = jnp.broadcast_to(row, (8, C))
    lane = lax.broadcasted_iota(jnp.int32, (8, C), 1)
    for by in (1, 2, 4):
        other = jnp.where(
            (lane & by) != 0, pltpu.roll(total, by, 1), pltpu.roll(total, C - by, 1)
        )
        total = total + other
    return total[0:1]


def packed(mean, spread):
    lane = lax.broadcasted_iota(jnp.int32, (1, C), 1)
    return jnp.where(lane % 2 == 0, mean, spread)


def unpacked(row):
    row = jnp.broadcast_to(row, (8, C))
    even = lax.broadcasted_iota(jnp.int32, (8, C), 1) % 2 == 0
    mean = jnp.where(even, row, pltpu.roll(row, 1, 1))
    spread = jnp.where(even, pltpu.roll(row, C - 1, 1), row)
    return mean[0:1], spread[0:1]


def merge(rows, count):
    means, squares = zip(*[unpacked(row) for row in rows])
    mean = sum(means) * (1.0 / len(means))
    spread = sum(squares) + float(count) * sum((m - mean) * (m - mean) for m in means)
    return mean, spread


def start_kernel(
    info_ref, gain_ref, shift_ref, x_ref, c_ref,
    xt_ref, ct_ref, send_ref, keep_ref, stat_ref, x_scr, c_scr, side_scr,
):
    place = info_ref[0]
    half = place // 2
    x = x_ref[0].astype(F32).T
    x_scr[...] = x
    xt_ref[...] = x.astype(BF16)
    mean = group_sum(jnp.sum(x, axis=0, keepdims=True)) * (1.0 / LOCAL)
    gap = x - mean
    spread = group_sum(jnp.sum(gap * gap, axis=0, keepdims=True))
    stat_ref[...] = jnp.broadcast_to(packed(mean, spread)[None], (N_FAR, 1, C))
    c = c_ref[0].astype(F32).T
    c_scr[...] = c
    ct_ref[...] = c.astype(BF16)
    zero = jnp.zeros((S, C), BF16)
    own = pl.ds(pl.multiple_of(place * ROWS, ROWS), ROWS)
    for kind, (scr, flat) in enumerate(((x_scr, xt_ref), (c_scr, ct_ref))):
        first, last = flat[0:S], flat[CELLS - S : CELLS]
        side_scr[kind, 0] = jnp.where(place == 0, first, zero)
        side_scr[kind, 2] = jnp.where(place == 3, last, zero)
        for side, column in ((1, S - 1), (3, 0)):
            side_scr[kind, side] = zero
            side_scr[kind, side, own, :] = scr[pl.ds(column, ROWS, stride=S), :].astype(BF16)
        send_ref[2, kind * S : (kind + 1) * S] = jnp.where(place == 1, last, first)
        for k in range(2):
            at = slice(kind * S, (kind + 1) * S)
            send_ref[k, at] = side_scr[kind, side_facing(info_ref, 2 - 2 * half + k)]
            keep_ref[k, at] = side_scr[kind, side_facing(info_ref, 2 * half + k)]


def middle_kernel(
    info_ref, keep_ref, in_ref, xt_ref, ct_ref, in_stat_ref, send_ref, left_ref, stat_ref
):
    odd = info_ref[0] % 2
    send_ref[0] = keep_ref[1 - odd] + in_ref[1 - odd]
    left_ref[...] = keep_ref[odd] + in_ref[odd]
    send_ref[2] = in_ref[2]
    stat_ref[...] = packed(*merge([in_stat_ref[k] for k in range(N_FAR)], LOCAL))[None]
    for kind, flat in enumerate((xt_ref, ct_ref)):
        send_ref[1, kind * S : (kind + 1) * S] = jnp.where(
            odd == 1, flat[0:S], flat[CELLS - S : CELLS]
        )


def side_facing(info_ref, direction):
    side = jnp.int32(0)
    for e in range(1, 4):
        side = jnp.where(info_ref[1 + e] % 4 == direction, e, side)
    return side


def side_parts(info_ref, side):
    first = jnp.where(side == 1, 2, jnp.where(side == 2, 6, 0))
    step = jnp.where(side % 2 == 1, 3, 1)
    start = jnp.where(side == 1, 1, jnp.where(side == 2, 3, 0))
    end = jnp.where(side == 0, 1, jnp.where(side == 3, 3, 2))
    mine = side % 2
    taps = [first, first + step, first + 2 * step]
    return taps, info_ref[5 + start] == mine, info_ref[5 + end] == mine


def flip_matrix():
    a = lax.broadcasted_iota(jnp.int32, (S, S), 0)
    b = lax.broadcasted_iota(jnp.int32, (S, S), 1)
    return jnp.where(a + b == S - 1, 1.0, 0.0).astype(BF16)


def turned(strip, flag):
    back = jnp.dot(flip_matrix(), strip, preferred_element_type=F32)
    return jnp.where(flag == 1, back, strip.astype(F32)).astype(BF16)


def seam_kernel(
    info_ref, keep_ref, in_ref, in_stat_ref, w_ref, message_ref, strips_ref, rows_ref, stat_ref,
):
    place = info_ref[0]
    odd = place % 2 == 1
    side = side_facing(info_ref, place)
    strips = keep_ref[...] + in_ref[0]
    strips_ref[...] = strips
    grads = strips[S : 2 * S]
    taps, at_start, at_end = side_parts(info_ref, side)
    parts = [jnp.dot(grads, w_ref[tap], preferred_element_type=F32) for tap in taps]
    row = lax.broadcasted_iota(jnp.int32, (S, C), 0)
    first, last = row == 0, row == S - 1
    grad = parts[1]
    grad = grad + jnp.where(last, 0.0, pltpu.roll(parts[0], S - 1, 0))
    grad = grad + jnp.where(first, 0.0, pltpu.roll(parts[2], 1, 0))
    grad = grad + jnp.where(first & at_start, parts[0], 0.0)
    grad = grad + jnp.where(last & at_end, parts[2], 0.0)
    message_ref[0:S] = strips[0:S]
    message_ref[S : 2 * S] = turned(grad.astype(BF16), info_ref[1 + side] // 4)
    direct, passed = in_ref[1], in_ref[2]
    above, below = jnp.where(odd, direct, passed), jnp.where(odd, passed, direct)
    zero = jnp.zeros((S, C), BF16)
    rows_ref[0:S] = above[0:S]
    rows_ref[S : 2 * S] = below[0:S]
    rows_ref[2 * S : 3 * S] = jnp.where(place == 0, zero, above[S : 2 * S])
    rows_ref[3 * S : 4 * S] = jnp.where(place == 3, zero, below[S : 2 * S])
    stat_ref[...] = jnp.broadcast_to(in_stat_ref[...], (N_NEAR, 1, C))


def main_kernel(
    info_ref, xt_ref, ct_ref, cot_ref, rows_ref, in_stat_ref, w_ref, gain_ref, shift_ref,
    strips_ref, in_ref, part_ref, pre_ref, norm_ref, weight_scr,
):
    place = info_ref[0]
    mean, spread = merge([in_stat_ref[k] for k in range(N_NEAR)], LOCAL * N_FAR)
    rstd = lax.rsqrt(spread * (1.0 / ENTRIES) + EPSILON)
    gain, shift = gain_ref[...], shift_ref[...]
    norm_ref[...] = jnp.concatenate([mean, rstd], axis=0)

    def affine(raw):
        normed = (raw.astype(F32) - mean) * rstd
        pre = normed * gain + shift
        return normed, pre, 1.0 / (1.0 + jnp.exp(-pre))

    def activated(raw):
        _, pre, sig = affine(raw)
        return (pre * sig).astype(BF16).astype(F32)

    wide = CELLS + 2 * S
    column = lax.broadcasted_iota(jnp.int32, (wide, C), 0) & (S - 1)
    starts, ends = column == 0, column == S - 1

    def beside(middle):
        before = jnp.where(starts, 0.0, pltpu.roll(middle, 1, 0))
        after = jnp.where(ends, 0.0, pltpu.roll(middle, wide - 1, 0))
        return before.astype(BF16), middle.astype(BF16), after.astype(BF16)

    top = jnp.where(place == 0, 0.0, activated(rows_ref[0:S]))
    bottom = jnp.where(place == 3, 0.0, activated(rows_ref[S : 2 * S]))
    normed, pre, sig = affine(xt_ref[...])
    own = (pre * sig).astype(BF16).astype(F32)
    windows = jnp.concatenate(beside(jnp.concatenate([top, own, bottom], axis=0)), axis=1)
    grad_out = cot_ref[0]
    for i in range(3):
        part = jnp.dot(grad_out, windows[i * S : i * S + CELLS], preferred_element_type=F32)
        for j in range(3):
            weight_scr[3 * i + j] = part[:, j * C : (j + 1) * C]

    side = side_facing(info_ref, place)
    taps, at_start, at_end = side_parts(info_ref, side)
    halo = activated(turned(in_ref[0:S], info_ref[1 + side] // 4)).astype(BF16)
    halo = jnp.concatenate([halo, halo], axis=0)
    strip = strips_ref[S : 2 * S].astype(F32)
    row = lax.broadcasted_iota(jnp.int32, (S, C), 0)
    first, last = row == 0, row == S - 1
    lines = (
        (jnp.where(last, 0.0, pltpu.roll(strip, S - 1, 0)), jnp.where(first & at_start, strip, 0.0)),
        (strip, jnp.zeros((S, C), F32)),
        (jnp.where(first, 0.0, pltpu.roll(strip, 1, 0)), jnp.where(last & at_end, strip, 0.0)),
    )
    for tap, pair in zip(taps, lines):
        weight_scr[tap] += lax.dot_general(
            jnp.concatenate(pair, axis=0).astype(BF16),
            halo,
            (((0,), (0,)), ((), ())),
            preferred_element_type=F32,
        )
    for tap in range(9):
        for h in range(2):
            part_ref[pl.ds(h * 9 + tap, 64, stride=CHUNK), :] = weight_scr[
                tap, h * 64 : (h + 1) * 64
            ]

    grads = jnp.concatenate(
        [rows_ref[2 * S : 3 * S], ct_ref[...], rows_ref[3 * S : 4 * S]], axis=0
    ).astype(F32)
    shifted = jnp.concatenate(beside(grads)[::-1], axis=1)
    act_grad = None
    for i in range(3):
        weight = jnp.concatenate([w_ref[3 * i + j] for j in range(3)], axis=0)
        term = jnp.dot(
            shifted[(2 - i) * S : (2 - i) * S + CELLS], weight, preferred_element_type=F32
        )
        act_grad = term if act_grad is None else act_grad + term
    pre_grad = act_grad * (sig * (1.0 + pre * (1.0 - sig)))
    pre_ref[...] = pre_grad
    gain_row = jnp.sum(pre_grad * normed, axis=0, keepdims=True)
    shift_row = jnp.sum(pre_grad, axis=0, keepdims=True)
    normed, pre, sig = affine(strips_ref[0:S])
    more = in_ref[S : 2 * S].astype(F32) * (sig * (1.0 + pre * (1.0 - sig)))
    gain_row = gain_row + jnp.sum(more * normed, axis=0, keepdims=True)
    shift_row = shift_row + jnp.sum(more, axis=0, keepdims=True)
    part_ref[pl.ds(18, 64, stride=CHUNK), :] = jnp.broadcast_to(gain_row, (64, C))
    part_ref[pl.ds(19, 64, stride=CHUNK), :] = jnp.broadcast_to(shift_row, (64, C))


def end_kernel(
    info_ref, pre_ref, xt_ref, norm_ref, gain_ref, shift_ref, total_ref, pair_ref, others_ref,
    out_ref, sums_ref, side_scr, more_scr,
):
    place = info_ref[0]
    base, odd = place // 2 * 2, place % 2
    for k in range(2):
        at = (odd + k) % 2
        side_scr[base + at] = pair_ref[k]
        side_scr[(base + 2) % 4 + at] = others_ref[k]
    own = pl.ds(pl.multiple_of(place * ROWS, ROWS), ROWS)
    more_scr[...] = jnp.zeros((CELLS, C), F32)
    more_scr[0:S] = jnp.where(place == 0, side_scr[info_ref[1] % 4].astype(F32), 0.0)
    more_scr[CELLS - S : CELLS] = jnp.where(place == 3, side_scr[info_ref[3] % 4].astype(F32), 0.0)
    for e, at in ((4, 0), (2, S - 1)):
        more_scr[pl.ds(at, ROWS, stride=S), :] += side_scr[info_ref[e] % 4, own, :].astype(F32)
    mean, rstd = norm_ref[0:1], norm_ref[1:2]
    gain = gain_ref[...]
    gain_total, shift_total = total_ref[18:19], total_ref[19:20]
    first = group_sum(gain * shift_total) * (1.0 / ENTRIES)
    second = group_sum(gain * gain_total) * (1.0 / ENTRIES)
    normed = (xt_ref[...].astype(F32) - mean) * rstd
    pre = normed * gain + shift_ref[...]
    sig = 1.0 / (1.0 + jnp.exp(-pre))
    pre_grad = pre_ref[...] + more_scr[...] * (sig * (1.0 + pre * (1.0 - sig)))
    out = rstd * (pre_grad * gain - first - normed * second)
    out_ref[0] = out.T.astype(BF16)
    sums_ref[...] = jnp.concatenate([gain_total, shift_total], axis=0) * SCALE


def weight_kernel(whole_ref, out_ref):
    for tap in range(9):
        for h in range(2):
            out_ref[tap, h * 64 : (h + 1) * 64] = (
                whole_ref[pl.ds(h * 9 + tap, 64, stride=CHUNK), :] * SCALE
            )


def sum_kernel(parts, copies, in_ref, out_ref):
    rows = in_ref.shape[0] // parts
    total = in_ref[0:rows]
    for k in range(1, parts):
        total = total + in_ref[k * rows : (k + 1) * rows]
    for k in range(copies):
        out_ref[k * rows : (k + 1) * rows] = total


def summed(x, parts, copies):
    rows = x.size // C
    return pl.pallas_call(
        functools.partial(sum_kernel, parts, copies),
        out_shape=shape((rows // parts * copies, C), F32),
        in_specs=[VMEM],
        out_specs=VMEM,
        compiler_params=PARAMS,
    )(x.reshape(rows, C))


def sum_and_pair_kernel(parts, copies, in_ref, own_ref, other_ref, out_ref, pair_ref):
    pair_ref[0] = own_ref[S : 2 * S]
    pair_ref[1] = other_ref[S : 2 * S]
    sum_kernel(parts, copies, in_ref, out_ref)


def exchanged(x, axes, parts):
    x = x.reshape(parts, x.shape[0] // parts // 4, 4, C)
    return lax.all_to_all(x, axes, 0, 0, tiled=True)


def shape(dims, dtype):
    return jax.ShapeDtypeStruct(dims, dtype)


def body(features, cotangent, conv_weight, norm_gain, norm_shift, seam_code, corner_map):
    place = lax.axis_index("zl").astype(jnp.int32).reshape(1)
    info = jnp.concatenate([place, seam_code[0], corner_map[0]])
    weight = conv_weight.transpose(1, 0, 2)
    gain, shift = norm_gain.reshape(1, C), norm_shift.reshape(1, C)
    xt, ct, send, keep, stats = pl.pallas_call(
        start_kernel,
        out_shape=(
            shape((CELLS, C), BF16),
            shape((CELLS, C), BF16),
            shape((3, LINE, C), BF16),
            shape((2, LINE, C), BF16),
            shape((N_FAR, 1, C), F32),
        ),
        in_specs=[SMEM] + [VMEM] * 4,
        out_specs=(VMEM,) * 5,
        scratch_shapes=[pltpu.VMEM((CELLS, C), F32)] * 2 + [pltpu.VMEM((2, 4, S, C), BF16)],
        compiler_params=PARAMS,
    )(info, gain, shift, features, cotangent)
    came = lax.ppermute(send, "zl", [(i, i ^ 2) for i in range(4)])
    stats = lax.all_to_all(stats, FAR, 0, 0, tiled=True)
    send, keep, stats = pl.pallas_call(
        middle_kernel,
        out_shape=(shape((3, LINE, C), BF16), shape((LINE, C), BF16), shape((1, 1, C), F32)),
        in_specs=[SMEM] + [VMEM] * 5,
        out_specs=(VMEM,) * 3,
        compiler_params=PARAMS,
    )(info, keep, came, xt, ct, stats)
    came = lax.ppermute(send, "zl", [(i, i ^ 1) for i in range(4)])
    message, strips, rows, stats = pl.pallas_call(
        seam_kernel,
        out_shape=(
            shape((LINE, C), BF16),
            shape((LINE, C), BF16),
            shape((2 * LINE, C), BF16),
            shape((N_NEAR, 1, C), F32),
        ),
        in_specs=[SMEM] + [VMEM] * 4,
        out_specs=(VMEM,) * 4,
        compiler_params=PARAMS,
    )(info, keep, came, stats, weight)
    message = lax.ppermute(
        message,
        tuple(AXES),
        [(4 * t + s, 4 * ((t + STEPS[s]) % 128) + (s + 2) % 4) for t in range(128) for s in range(4)],
    )
    stats = lax.all_to_all(stats, NEAR, 0, 0, tiled=True)
    parts, pre_grad, norm = pl.pallas_call(
        main_kernel,
        out_shape=(
            shape((64 * CHUNK, C), F32),
            shape((CELLS, C), F32),
            shape((2, C), F32),
        ),
        in_specs=[SMEM] + [VMEM] * 10,
        out_specs=(VMEM,) * 3,
        scratch_shapes=[pltpu.VMEM((9, C, C), F32)],
        compiler_params=PARAMS,
    )(info, xt, ct, cotangent, rows, stats, weight, gain, shift, strips, message)
    other = lax.ppermute(message, "zl", [(i, i ^ 1) for i in range(4)])
    parts = summed(exchanged(parts, "co", 2), 2, 1)
    parts, pair = pl.pallas_call(
        functools.partial(sum_and_pair_kernel, N_FAR, 8),
        out_shape=(shape((8 * CHUNK, C), F32), shape((2, S, C), BF16)),
        in_specs=[VMEM] * 3,
        out_specs=(VMEM,) * 2,
        compiler_params=PARAMS,
    )(exchanged(parts, FAR, N_FAR).reshape(N_FAR * CHUNK, C), message, other)
    others = lax.ppermute(pair, "zl", [(i, i ^ 2) for i in range(4)])
    parts = summed(exchanged(parts, ("zh", "zl"), 8), 8, N_FAR)
    half = exchanged(parts, FAR, N_FAR)
    whole = lax.all_gather(half, "co", axis=0, tiled=True)
    grad_input, sums = pl.pallas_call(
        end_kernel,
        out_shape=(shape((1, C, CELLS), BF16), shape((2, C), F32)),
        in_specs=[SMEM] + [VMEM] * 8,
        out_specs=(VMEM,) * 2,
        scratch_shapes=[pltpu.VMEM((4, S, C), BF16), pltpu.VMEM((CELLS, C), F32)],
        compiler_params=PARAMS,
    )(info, pre_grad, xt, norm, gain, shift, parts, pair, others)
    grad_weight = pl.pallas_call(
        weight_kernel,
        out_shape=shape((9, C, C), F32),
        in_specs=[VMEM],
        out_specs=VMEM,
        compiler_params=PARAMS,
    )(whole.reshape(64 * CHUNK, C)).transpose(1, 0, 2)
    return grad_input, grad_weight, sums[0], sums[1]


def solution(mesh):
    fine = Mesh(mesh.devices.reshape(tuple(AXES.values())), tuple(AXES))
    return jax.shard_map(
        body,
        mesh=fine,
        in_specs=(
            P(TILE, None, "zl"),
            P(TILE, None, "zl"),
            P(),
            P(),
            P(),
            P(TILE, None),
            P(TILE, None),
        ),
        out_specs=(P(TILE, None, "zl"), P(), P(), P()),
        check_vma=False,
    )
```

```python
import functools
import math

import jax
import jax.numpy as jnp
from jax import lax
from jax.experimental import pallas as pl
from jax.experimental.pallas import tpu as pltpu
from jax.sharding import Mesh
from jax.sharding import PartitionSpec as P

GC = 4
S = 64
PER_GROUP = 8
EPSILON = 1e-05
STEPS = (-GC, 1, GC, -1)
ROWS = 16
CELLS = ROWS * S
C = 128
LINE = 2 * S
EDGE = 2 * S + 2 * ROWS
CHUNK = 20

TILE = ("y", "x", "zh", "co")
AXES = {"y": 8, "x": 4, "zh": 2, "co": 2, "z2": 2, "z1": 2}
SUB = ("z2", "z1")
NEAR = ("zh", "co", "z2", "z1")
FAR = ("y", "x")
N_NEAR = 16
N_FAR = 32
DEVICES = 512
ENTRIES = DEVICES * CELLS * PER_GROUP
LOCAL = CELLS * PER_GROUP
SCALE = 1.0 / math.sqrt(DEVICES * CELLS)

F32 = jnp.float32
BF16 = jnp.bfloat16
VMEM = pl.BlockSpec(memory_space=pltpu.VMEM)
SMEM = pl.BlockSpec(memory_space=pltpu.SMEM)
PARAMS = pltpu.CompilerParams(vmem_limit_bytes=40 * 1024 * 1024)


def group_sum(row):
    total = jnp.broadcast_to(row, (8, C))
    lane = lax.broadcasted_iota(jnp.int32, (8, C), 1)
    for by in (1, 2, 4):
        other = jnp.where(
            (lane & by) != 0, pltpu.roll(total, by, 1), pltpu.roll(total, C - by, 1)
        )
        total = total + other
    return total[0:1]


def packed(mean, spread):
    lane = lax.broadcasted_iota(jnp.int32, (1, C), 1)
    return jnp.where(lane % 2 == 0, mean, spread)


def unpacked(row):
    row = jnp.broadcast_to(row, (8, C))
    even = lax.broadcasted_iota(jnp.int32, (8, C), 1) % 2 == 0
    mean = jnp.where(even, row, pltpu.roll(row, 1, 1))
    spread = jnp.where(even, pltpu.roll(row, C - 1, 1), row)
    return mean[0:1], spread[0:1]


def merge(rows, count):
    means, squares = zip(*[unpacked(row) for row in rows])
    mean = sum(means) * (1.0 / len(means))
    spread = sum(squares) + float(count) * sum((m - mean) * (m - mean) for m in means)
    return mean, spread


def start_kernel(x_ref, c_ref, xt_ref, ct_ref, edge_ref, stat_ref, x_scr, c_scr):
    x = x_ref[0].astype(F32).T
    x_scr[...] = x
    xt_ref[...] = x.astype(BF16)
    c = c_ref[0].astype(F32).T
    c_scr[...] = c
    ct_ref[...] = c.astype(BF16)
    for kind, (scr, flat) in enumerate(((x_scr, xt_ref), (c_scr, ct_ref))):
        edge_ref[kind, 0:S] = flat[0:S]
        edge_ref[kind, S : 2 * S] = flat[CELLS - S : CELLS]
        for k, column in enumerate((S - 1, 0)):
            edge_ref[kind, 2 * S + k * ROWS : 2 * S + (k + 1) * ROWS] = scr[
                pl.ds(column, ROWS, stride=S), :
            ].astype(BF16)
    mean = group_sum(jnp.sum(x, axis=0, keepdims=True)) * (1.0 / LOCAL)
    gap = x - mean
    spread = group_sum(jnp.sum(gap * gap, axis=0, keepdims=True))
    stat_ref[...] = jnp.broadcast_to(packed(mean, spread)[None], (N_FAR, 1, C))


def middle_kernel(
    info_ref, own_ref, other_ref, gain_ref, shift_ref,
    send_ref, left_ref, affine_ref, side_scr,
):
    place = info_ref[0]
    odd = place % 2
    pair = (place + 2) % 4
    affine_ref[0:1], affine_ref[1:2] = gain_ref[...], shift_ref[...]
    zero = jnp.zeros((S, C), BF16)
    first, last = slice(0, S), slice(S, 2 * S)
    for kind in range(2):
        side_scr[kind, 0] = jnp.where(
            place == 0, own_ref[kind, first], jnp.where(pair == 0, other_ref[kind, first], zero)
        )
        side_scr[kind, 2] = jnp.where(
            place == 3, own_ref[kind, last], jnp.where(pair == 3, other_ref[kind, last], zero)
        )
        for k, side in enumerate((1, 3)):
            at = slice(2 * S + k * ROWS, 2 * S + (k + 1) * ROWS)
            side_scr[kind, side] = zero
            for who, ref in ((place, own_ref), (pair, other_ref)):
                rows = pl.ds(pl.multiple_of(who * ROWS, ROWS), ROWS)
                side_scr[kind, side, rows, :] = ref[kind, at]
        here = slice(kind * S, (kind + 1) * S)
        send_ref[0, here] = side_scr[kind, side_facing(info_ref, place + 1 - 2 * odd)]
        left_ref[here] = side_scr[kind, side_facing(info_ref, place)]
        send_ref[1, here] = jnp.where(odd == 1, own_ref[kind, first], own_ref[kind, last])
        send_ref[2, here] = jnp.where(place == 0, other_ref[kind, first], other_ref[kind, last])


def side_facing(info_ref, direction):
    side = jnp.int32(0)
    for e in range(1, 4):
        side = jnp.where(info_ref[1 + e] % 4 == direction, e, side)
    return side


def side_parts(info_ref, side):
    first = jnp.where(side == 1, 2, jnp.where(side == 2, 6, 0))
    step = jnp.where(side % 2 == 1, 3, 1)
    start = jnp.where(side == 1, 1, jnp.where(side == 2, 3, 0))
    end = jnp.where(side == 0, 1, jnp.where(side == 3, 3, 2))
    mine = side % 2
    taps = [first, first + step, first + 2 * step]
    return taps, info_ref[5 + start] == mine, info_ref[5 + end] == mine


def flip_matrix():
    a = lax.broadcasted_iota(jnp.int32, (S, S), 0)
    b = lax.broadcasted_iota(jnp.int32, (S, S), 1)
    return jnp.where(a + b == S - 1, 1.0, 0.0).astype(BF16)


def turned(strip, flag):
    back = jnp.dot(flip_matrix(), strip, preferred_element_type=F32)
    return jnp.where(flag == 1, back, strip.astype(F32)).astype(BF16)


def seam_kernel(
    info_ref, keep_ref, in_ref, in_stat_ref, w_ref, message_ref, strips_ref, rows_ref, stat_ref,
):
    place = info_ref[0]
    odd = place % 2 == 1
    side = side_facing(info_ref, place)
    other = 1 - place % 2
    strips = keep_ref[...] + in_ref[other, 0]
    strips_ref[...] = strips
    grads = strips[S : 2 * S]
    taps, at_start, at_end = side_parts(info_ref, side)
    parts = [jnp.dot(grads, w_ref[tap], preferred_element_type=F32) for tap in taps]
    row = lax.broadcasted_iota(jnp.int32, (S, C), 0)
    first, last = row == 0, row == S - 1
    grad = parts[1]
    grad = grad + jnp.where(last, 0.0, pltpu.roll(parts[0], S - 1, 0))
    grad = grad + jnp.where(first, 0.0, pltpu.roll(parts[2], 1, 0))
    grad = grad + jnp.where(first & at_start, parts[0], 0.0)
    grad = grad + jnp.where(last & at_end, parts[2], 0.0)
    message_ref[0:S] = strips[0:S]
    message_ref[S : 2 * S] = turned(grad.astype(BF16), info_ref[1 + side] // 4)
    direct, passed = in_ref[other, 1], in_ref[other, 2]
    above, below = jnp.where(odd, direct, passed), jnp.where(odd, passed, direct)
    zero = jnp.zeros((S, C), BF16)
    rows_ref[0:S] = above[0:S]
    rows_ref[S : 2 * S] = below[0:S]
    rows_ref[2 * S : 3 * S] = jnp.where(place == 0, zero, above[S : 2 * S])
    rows_ref[3 * S : 4 * S] = jnp.where(place == 3, zero, below[S : 2 * S])
    stats = packed(*merge([in_stat_ref[k] for k in range(N_FAR)], LOCAL))
    stat_ref[...] = jnp.broadcast_to(stats[None], (N_NEAR, 1, C))


def main_kernel(
    info_ref, xt_ref, ct_ref, cot_ref, rows_ref, in_stat_ref, w_ref, affine_ref,
    strips_ref, in_ref, keep_ref, send_ref, pre_ref, norm_ref, weight_scr,
):
    place = info_ref[0]
    mean, spread = merge([in_stat_ref[k] for k in range(N_NEAR)], LOCAL * N_FAR)
    rstd = lax.rsqrt(spread * (1.0 / ENTRIES) + EPSILON)
    gain, shift = affine_ref[0:1], affine_ref[1:2]
    norm_ref[...] = jnp.concatenate([mean, rstd], axis=0)

    def affine(raw):
        normed = (raw.astype(F32) - mean) * rstd
        pre = normed * gain + shift
        return normed, pre, 1.0 / (1.0 + jnp.exp(-pre))

    def activated(raw):
        _, pre, sig = affine(raw)
        return (pre * sig).astype(BF16).astype(F32)

    wide = CELLS + 2 * S
    column = lax.broadcasted_iota(jnp.int32, (wide, C), 0) & (S - 1)
    starts, ends = column == 0, column == S - 1

    def beside(middle):
        before = jnp.where(starts, 0.0, pltpu.roll(middle, 1, 0))
        after = jnp.where(ends, 0.0, pltpu.roll(middle, wide - 1, 0))
        return before.astype(BF16), middle.astype(BF16), after.astype(BF16)

    top = jnp.where(place == 0, 0.0, activated(rows_ref[0:S]))
    bottom = jnp.where(place == 3, 0.0, activated(rows_ref[S : 2 * S]))
    normed, pre, sig = affine(xt_ref[...])
    own = (pre * sig).astype(BF16).astype(F32)
    windows = jnp.concatenate(beside(jnp.concatenate([top, own, bottom], axis=0)), axis=1)
    grad_out = cot_ref[0]
    for i in range(3):
        part = jnp.dot(grad_out, windows[i * S : i * S + CELLS], preferred_element_type=F32)
        for j in range(3):
            weight_scr[3 * i + j] = part[:, j * C : (j + 1) * C]

    side = side_facing(info_ref, place)
    taps, at_start, at_end = side_parts(info_ref, side)
    halo = activated(turned(in_ref[0:S], info_ref[1 + side] // 4)).astype(BF16)
    halo = jnp.concatenate([halo, halo], axis=0)
    strip = strips_ref[S : 2 * S].astype(F32)
    row = lax.broadcasted_iota(jnp.int32, (S, C), 0)
    first, last = row == 0, row == S - 1
    lines = (
        (jnp.where(last, 0.0, pltpu.roll(strip, S - 1, 0)), jnp.where(first & at_start, strip, 0.0)),
        (strip, jnp.zeros((S, C), F32)),
        (jnp.where(first, 0.0, pltpu.roll(strip, 1, 0)), jnp.where(last & at_end, strip, 0.0)),
    )
    for tap, pair in zip(taps, lines):
        weight_scr[tap] += lax.dot_general(
            jnp.concatenate(pair, axis=0).astype(BF16),
            halo,
            (((0,), (0,)), ((), ())),
            preferred_element_type=F32,
        )
    core = info_ref[9]

    def put(row, low, high):
        at = pl.ds(row, N_FAR, stride=CHUNK)
        keep_ref[at, :] = jnp.where(core == 0, low, high)
        send_ref[at, :] = jnp.where(core == 0, high, low)

    for tap in range(9):
        for h in range(2):
            put(
                h * 9 + tap,
                weight_scr[tap, h * 64 : h * 64 + 32],
                weight_scr[tap, h * 64 + 32 : (h + 1) * 64],
            )

    grads = jnp.concatenate(
        [rows_ref[2 * S : 3 * S], ct_ref[...], rows_ref[3 * S : 4 * S]], axis=0
    ).astype(F32)
    shifted = jnp.concatenate(beside(grads)[::-1], axis=1)
    act_grad = None
    for i in range(3):
        weight = jnp.concatenate([w_ref[3 * i + j] for j in range(3)], axis=0)
        term = jnp.dot(
            shifted[(2 - i) * S : (2 - i) * S + CELLS], weight, preferred_element_type=F32
        )
        act_grad = term if act_grad is None else act_grad + term
    pre_grad = act_grad * (sig * (1.0 + pre * (1.0 - sig)))
    pre_ref[...] = pre_grad
    gain_row = jnp.sum(pre_grad * normed, axis=0, keepdims=True)
    shift_row = jnp.sum(pre_grad, axis=0, keepdims=True)
    normed, pre, sig = affine(strips_ref[0:S])
    more = in_ref[S : 2 * S].astype(F32) * (sig * (1.0 + pre * (1.0 - sig)))
    gain_row = gain_row + jnp.sum(more * normed, axis=0, keepdims=True)
    shift_row = shift_row + jnp.sum(more, axis=0, keepdims=True)
    for k, row in ((18, gain_row), (19, shift_row)):
        row = jnp.broadcast_to(row, (N_FAR, C))
        put(k, row, row)


def end_kernel(
    info_ref, pre_ref, xt_ref, norm_ref, affine_ref, total_ref, pair_ref, others_ref,
    out_ref, gain_sum_ref, shift_sum_ref, side_scr, more_scr,
):
    place = info_ref[0]
    base, odd = place // 2 * 2, place % 2
    for k in range(2):
        at = (odd + k) % 2
        side_scr[base + at] = pair_ref[k]
        side_scr[(base + 2) % 4 + at] = others_ref[k]
    own = pl.ds(pl.multiple_of(place * ROWS, ROWS), ROWS)
    more_scr[...] = jnp.zeros((CELLS, C), F32)
    more_scr[0:S] = jnp.where(place == 0, side_scr[info_ref[1] % 4].astype(F32), 0.0)
    more_scr[CELLS - S : CELLS] = jnp.where(place == 3, side_scr[info_ref[3] % 4].astype(F32), 0.0)
    for e, at in ((4, 0), (2, S - 1)):
        more_scr[pl.ds(at, ROWS, stride=S), :] += side_scr[info_ref[e] % 4, own, :].astype(F32)
    mean, rstd = norm_ref[0:1], norm_ref[1:2]
    gain, shift = affine_ref[0:1], affine_ref[1:2]
    gain_total, shift_total = total_ref[18:19], total_ref[19:20]
    first = group_sum(gain * shift_total) * (1.0 / ENTRIES)
    second = group_sum(gain * gain_total) * (1.0 / ENTRIES)
    normed = (xt_ref[...].astype(F32) - mean) * rstd
    pre = normed * gain + shift
    sig = 1.0 / (1.0 + jnp.exp(-pre))
    pre_grad = pre_ref[...] + more_scr[...] * (sig * (1.0 + pre * (1.0 - sig)))
    out = rstd * (pre_grad * gain - first - normed * second)
    out_ref[0] = out.T.astype(BF16)
    gain_sum_ref[...] = gain_total * SCALE
    shift_sum_ref[...] = shift_total * SCALE


def weight_kernel(whole_ref, out_ref):
    for tap in range(9):
        for h in range(2):
            out_ref[tap, h * 64 : (h + 1) * 64] = (
                whole_ref[pl.ds(h * 9 + tap, 64, stride=CHUNK), :] * SCALE
            )


def sum_kernel(parts, copies, in_ref, out_ref):
    rows = in_ref.shape[0] // parts
    total = in_ref[0:rows]
    for k in range(1, parts):
        total = total + in_ref[k * rows : (k + 1) * rows]
    for k in range(copies):
        out_ref[k * rows : (k + 1) * rows] = total


def add_kernel(a_ref, b_ref, out_ref):
    out_ref[...] = a_ref[...] + b_ref[...]


def summed(x, parts, copies):
    rows = x.size // C
    return pl.pallas_call(
        functools.partial(sum_kernel, parts, copies),
        out_shape=shape((rows // parts * copies, C), F32),
        in_specs=[VMEM],
        out_specs=VMEM,
        compiler_params=PARAMS,
    )(x.reshape(rows, C))


def sum_and_pair_kernel(parts, copies, in_ref, own_ref, other_ref, out_ref, pair_ref):
    pair_ref[0] = own_ref[S : 2 * S]
    pair_ref[1] = other_ref[S : 2 * S]
    sum_kernel(parts, copies, in_ref, out_ref)


def exchanged(x, axes, parts):
    x = x.reshape(parts, x.shape[0] // parts // 4, 4, C)
    return lax.all_to_all(x, axes, 0, 0, tiled=True)


def shape(dims, dtype):
    return jax.ShapeDtypeStruct(dims, dtype)


def body(features, cotangent, conv_weight, norm_gain, norm_shift, seam_code, corner_map):
    place = lax.axis_index(SUB).astype(jnp.int32).reshape(1)
    core = lax.axis_index("co").astype(jnp.int32).reshape(1)
    info = jnp.concatenate([place, seam_code[0], corner_map[0], core])
    weight = conv_weight.transpose(1, 0, 2)
    gain, shift = norm_gain.reshape(1, C), norm_shift.reshape(1, C)
    xt, ct, edges, stats = pl.pallas_call(
        start_kernel,
        out_shape=(
            shape((CELLS, C), BF16),
            shape((CELLS, C), BF16),
            shape((2, EDGE, C), BF16),
            shape((N_FAR, 1, C), F32),
        ),
        in_specs=[VMEM] * 2,
        out_specs=(VMEM,) * 4,
        scratch_shapes=[pltpu.VMEM((CELLS, C), F32)] * 2,
        compiler_params=PARAMS,
    )(features, cotangent)
    came = lax.ppermute(edges, "z2", [(0, 1), (1, 0)])
    stats = lax.all_to_all(stats, FAR, 0, 0, tiled=True)
    send, keep, affine = pl.pallas_call(
        middle_kernel,
        out_shape=(
            shape((3, LINE, C), BF16),
            shape((LINE, C), BF16),
            shape((2, C), F32),
        ),
        in_specs=[SMEM] + [VMEM] * 4,
        out_specs=(VMEM,) * 3,
        scratch_shapes=[pltpu.VMEM((2, 4, S, C), BF16)],
        compiler_params=PARAMS,
    )(info, edges, came, gain, shift)
    came = lax.all_gather(send, "z1", axis=0, tiled=False)
    message, strips, rows, stats = pl.pallas_call(
        seam_kernel,
        out_shape=(
            shape((LINE, C), BF16),
            shape((LINE, C), BF16),
            shape((2 * LINE, C), BF16),
            shape((N_NEAR, 1, C), F32),
        ),
        in_specs=[SMEM] + [VMEM] * 4,
        out_specs=(VMEM,) * 4,
        compiler_params=PARAMS,
    )(info, keep, came, stats, weight)
    message = lax.ppermute(
        message,
        tuple(AXES),
        [(4 * t + s, 4 * ((t + STEPS[s]) % 128) + (s + 2) % 4) for t in range(128) for s in range(4)],
    )
    stats = lax.all_to_all(stats, NEAR, 0, 0, tiled=True)
    parts, send, pre_grad, norm = pl.pallas_call(
        main_kernel,
        out_shape=(
            shape((N_FAR * CHUNK, C), F32),
            shape((N_FAR * CHUNK, C), F32),
            shape((CELLS, C), F32),
            shape((2, C), F32),
        ),
        in_specs=[SMEM] + [VMEM] * 9,
        out_specs=(VMEM,) * 4,
        scratch_shapes=[pltpu.VMEM((9, C, C), F32)],
        compiler_params=PARAMS,
    )(info, xt, ct, cotangent, rows, stats, weight, affine, strips, message)
    other = lax.ppermute(message, "z1", [(0, 1), (1, 0)])
    send = lax.ppermute(send, "co", [(0, 1), (1, 0)])
    parts = pl.pallas_call(
        add_kernel,
        out_shape=shape((N_FAR * CHUNK, C), F32),
        in_specs=[VMEM] * 2,
        out_specs=VMEM,
        compiler_params=PARAMS,
    )(parts, send)
    parts, pair = pl.pallas_call(
        functools.partial(sum_and_pair_kernel, N_FAR, 8),
        out_shape=(shape((8 * CHUNK, C), F32), shape((2, S, C), BF16)),
        in_specs=[VMEM] * 3,
        out_specs=(VMEM,) * 2,
        compiler_params=PARAMS,
    )(exchanged(parts, FAR, N_FAR).reshape(N_FAR * CHUNK, C), message, other)
    others = lax.ppermute(pair, "z2", [(0, 1), (1, 0)])
    parts = summed(exchanged(parts, ("zh", "z2", "z1"), 8), 8, N_FAR)
    half = exchanged(parts, FAR, N_FAR)
    whole = lax.all_gather(half, "co", axis=0, tiled=True)
    grad_input, grad_gain, grad_shift = pl.pallas_call(
        end_kernel,
        out_shape=(shape((1, C, CELLS), BF16), shape((1, C), F32), shape((1, C), F32)),
        in_specs=[SMEM] + [VMEM] * 7,
        out_specs=(VMEM,) * 3,
        scratch_shapes=[pltpu.VMEM((4, S, C), BF16), pltpu.VMEM((CELLS, C), F32)],
        compiler_params=PARAMS,
    )(info, pre_grad, xt, norm, affine, parts, pair, others)
    grad_weight = pl.pallas_call(
        weight_kernel,
        out_shape=shape((9, C, C), F32),
        in_specs=[VMEM],
        out_specs=VMEM,
        compiler_params=PARAMS,
    )(whole.reshape(64 * CHUNK, C)).transpose(1, 0, 2)
    return grad_input, grad_weight, grad_gain.reshape(C), grad_shift.reshape(C)


def solution(mesh):
    fine = Mesh(mesh.devices.reshape(tuple(AXES.values())), tuple(AXES))
    return jax.shard_map(
        body,
        mesh=fine,
        in_specs=(
            P(TILE, None, SUB),
            P(TILE, None, SUB),
            P(),
            P(),
            P(),
            P(TILE, None),
            P(TILE, None),
        ),
        out_specs=(P(TILE, None, SUB), P(), P(), P()),
        check_vma=False,
    )
```

```python
import functools
import math

import jax
import jax.numpy as jnp
from jax import lax
from jax.experimental import pallas as pl
from jax.experimental.pallas import tpu as pltpu
from jax.sharding import Mesh
from jax.sharding import PartitionSpec as P

GC = 4
S = 64
PER_GROUP = 8
EPSILON = 1e-05
STEPS = (-GC, 1, GC, -1)
ROWS = 16
CELLS = ROWS * S
C = 128
LINE = 2 * S
EDGE = 2 * S + 2 * ROWS
CHUNK = 20

TILE = ("y", "x", "zh", "co")
AXES = {"y": 8, "x": 4, "zh": 2, "co": 2, "z2": 2, "z1": 2}
SUB = ("z2", "z1")
NEAR = ("zh", "co", "z2", "z1")
FAR = ("y", "x")
N_NEAR = 16
N_FAR = 32
DEVICES = 512
ENTRIES = DEVICES * CELLS * PER_GROUP
LOCAL = CELLS * PER_GROUP
SCALE = 1.0 / math.sqrt(DEVICES * CELLS)

F32 = jnp.float32
BF16 = jnp.bfloat16
VMEM = pl.BlockSpec(memory_space=pltpu.VMEM)
SMEM = pl.BlockSpec(memory_space=pltpu.SMEM)
START_VMEM = 56098816
PARAMS = pltpu.CompilerParams(vmem_limit_bytes=40 * 1024 * 1024)


def group_sum(row):
    total = jnp.broadcast_to(row, (8, C))
    lane = lax.broadcasted_iota(jnp.int32, (8, C), 1)
    for by in (1, 2, 4):
        other = jnp.where(
            (lane & by) != 0, pltpu.roll(total, by, 1), pltpu.roll(total, C - by, 1)
        )
        total = total + other
    return total[0:1]


def packed(mean, spread):
    lane = lax.broadcasted_iota(jnp.int32, (1, C), 1)
    return jnp.where(lane % 2 == 0, mean, spread)


def unpacked(row):
    row = jnp.broadcast_to(row, (8, C))
    even = lax.broadcasted_iota(jnp.int32, (8, C), 1) % 2 == 0
    mean = jnp.where(even, row, pltpu.roll(row, 1, 1))
    spread = jnp.where(even, pltpu.roll(row, C - 1, 1), row)
    return mean[0:1], spread[0:1]


def merge(rows, count):
    means, squares = zip(*[unpacked(row) for row in rows])
    mean = sum(means) * (1.0 / len(means))
    spread = sum(squares) + float(count) * sum((m - mean) * (m - mean) for m in means)
    return mean, spread


def start_kernel(
    x_hbm, c_hbm, xt_ref, ct_ref, edge_ref, stat_ref, x_in, c_in, x_scr, c_scr, sems
):
    copies = []
    for kind, (far, near) in enumerate(((x_hbm, x_in), (c_hbm, c_in))):
        for k in range(4):
            at = pl.ds(k * 32, 32)
            copies.append(pltpu.make_async_copy(far.at[0, at], near.at[at], sems.at[kind, k]))
            copies[-1].start()
    for copy in copies[:4]:
        copy.wait()
    x = x_in[...].astype(F32).T
    x_scr[...] = x
    xt_ref[...] = x.astype(BF16)
    for copy in copies[4:]:
        copy.wait()
    c = c_in[...].astype(F32).T
    c_scr[...] = c
    ct_ref[...] = c.astype(BF16)
    for kind, (scr, flat) in enumerate(((x_scr, xt_ref), (c_scr, ct_ref))):
        edge_ref[kind, 0:S] = flat[0:S]
        edge_ref[kind, S : 2 * S] = flat[CELLS - S : CELLS]
        for k, column in enumerate((S - 1, 0)):
            edge_ref[kind, 2 * S + k * ROWS : 2 * S + (k + 1) * ROWS] = scr[
                pl.ds(column, ROWS, stride=S), :
            ].astype(BF16)
    mean = group_sum(jnp.sum(x, axis=0, keepdims=True)) * (1.0 / LOCAL)
    gap = x - mean
    spread = group_sum(jnp.sum(gap * gap, axis=0, keepdims=True))
    stat_ref[...] = jnp.broadcast_to(packed(mean, spread)[None], (N_FAR, 1, C))


def corners_of(info_ref, side):
    start = jnp.where(side == 1, 1, jnp.where(side == 2, 3, 0))
    end = jnp.where(side == 0, 1, jnp.where(side == 3, 3, 2))
    return info_ref[5 + start] == side % 2, info_ref[5 + end] == side % 2


TAPS = ((0, 1, 2), (2, 5, 8), (6, 7, 8), (0, 3, 6))
FIRST, LAST, CORE, SIDE, AT_START, AT_END, BACK, ODD = 0, 1, 2, 3, 7, 8, 9, 10


def middle_kernel(
    info_ref, own_ref, other_ref, gain_ref, shift_ref,
    send_ref, left_ref, affine_ref, mark_ref, side_scr,
):
    place = info_ref[0]
    odd = place % 2
    pair = (place + 2) % 4
    affine_ref[0:1], affine_ref[1:2] = gain_ref[...], shift_ref[...]
    mine = side_facing(info_ref, place)
    at_start, at_end = corners_of(info_ref, mine)
    marks = (
        [place == 0, place == 3, info_ref[9] == 1]
        + [mine == e for e in range(4)]
        + [at_start, at_end, info_ref[1 + mine] // 4 == 1, odd == 1]
    )
    for k, mark in enumerate(marks):
        mark_ref[k : k + 1] = jnp.full((1, C), jnp.where(mark, 1.0, 0.0), F32)
    zero = jnp.zeros((S, C), BF16)
    first, last = slice(0, S), slice(S, 2 * S)
    for kind in range(2):
        side_scr[kind, 0] = jnp.where(
            place == 0, own_ref[kind, first], jnp.where(pair == 0, other_ref[kind, first], zero)
        )
        side_scr[kind, 2] = jnp.where(
            place == 3, own_ref[kind, last], jnp.where(pair == 3, other_ref[kind, last], zero)
        )
        for k, side in enumerate((1, 3)):
            at = slice(2 * S + k * ROWS, 2 * S + (k + 1) * ROWS)
            side_scr[kind, side] = zero
            for who, ref in ((place, own_ref), (pair, other_ref)):
                rows = pl.ds(pl.multiple_of(who * ROWS, ROWS), ROWS)
                side_scr[kind, side, rows, :] = ref[kind, at]
        here = slice(kind * S, (kind + 1) * S)
        send_ref[0, here] = side_scr[kind, side_facing(info_ref, place + 1 - 2 * odd)]
        left_ref[here] = side_scr[kind, side_facing(info_ref, place)]
        send_ref[1, here] = jnp.where(odd == 1, own_ref[kind, first], own_ref[kind, last])
        send_ref[2, here] = jnp.where(place == 0, other_ref[kind, first], other_ref[kind, last])


def side_facing(info_ref, direction):
    side = jnp.int32(0)
    for e in range(1, 4):
        side = jnp.where(info_ref[1 + e] % 4 == direction, e, side)
    return side


def flip_matrix():
    a = lax.broadcasted_iota(jnp.int32, (S, S), 0)
    b = lax.broadcasted_iota(jnp.int32, (S, S), 1)
    return jnp.where(a + b == S - 1, 1.0, 0.0).astype(BF16)


def turned(strip, flag):
    back = jnp.dot(flip_matrix(), strip, preferred_element_type=F32)
    return jnp.where(flag, back, strip.astype(F32)).astype(BF16)


def seam_kernel(
    mark_ref, keep_ref, in_ref, in_stat_ref, w_ref, message_ref, strips_ref, rows_ref, stat_ref,
):
    def mark(k):
        return mark_ref[k : k + 1] > 0.5

    def other(k):
        return jnp.where(mark(ODD), in_ref[0, k].astype(F32), in_ref[1, k].astype(F32))

    strips = (keep_ref[...].astype(F32) + other(0)).astype(BF16)
    strips_ref[...] = strips
    grads = strips[S : 2 * S]
    parts = []
    for k in range(3):
        weight = w_ref[TAPS[0][k]].astype(F32)
        for e in range(1, 4):
            weight = jnp.where(mark(SIDE + e), w_ref[TAPS[e][k]].astype(F32), weight)
        parts.append(jnp.dot(grads, weight.astype(BF16), preferred_element_type=F32))
    row = lax.broadcasted_iota(jnp.int32, (S, C), 0)
    first, last = row == 0, row == S - 1
    grad = parts[1]
    grad = grad + jnp.where(last, 0.0, pltpu.roll(parts[0], S - 1, 0))
    grad = grad + jnp.where(first, 0.0, pltpu.roll(parts[2], 1, 0))
    grad = grad + jnp.where(first & mark(AT_START), parts[0], 0.0)
    grad = grad + jnp.where(last & mark(AT_END), parts[2], 0.0)
    message_ref[0:S] = strips[0:S]
    message_ref[S : 2 * S] = turned(grad.astype(BF16), mark(BACK))
    direct, passed = other(1), other(2)
    above = jnp.where(mark(ODD), direct, passed)
    below = jnp.where(mark(ODD), passed, direct)
    rows_ref[0:S] = above[0:S].astype(BF16)
    rows_ref[S : 2 * S] = below[0:S].astype(BF16)
    rows_ref[2 * S : 3 * S] = jnp.where(mark(FIRST), 0.0, above[S : 2 * S]).astype(BF16)
    rows_ref[3 * S : 4 * S] = jnp.where(mark(LAST), 0.0, below[S : 2 * S]).astype(BF16)
    stats = packed(*merge([in_stat_ref[k] for k in range(N_FAR)], LOCAL))
    stat_ref[...] = jnp.broadcast_to(stats[None], (N_NEAR, 1, C))


def beside(middle):
    wide = middle.shape[0]
    column = lax.broadcasted_iota(jnp.int32, middle.shape, 0) & (S - 1)
    before = jnp.where(column == 0, 0.0, pltpu.roll(middle, 1, 0))
    after = jnp.where(column == S - 1, 0.0, pltpu.roll(middle, wide - 1, 0))
    return before.astype(BF16), middle.astype(BF16), after.astype(BF16)


def grad_kernel(ct_ref, rows_ref, w_ref, out_ref):
    grads = jnp.concatenate(
        [rows_ref[2 * S : 3 * S], ct_ref[...], rows_ref[3 * S : 4 * S]], axis=0
    ).astype(F32)
    shifted = jnp.concatenate(beside(grads)[::-1], axis=1)
    act_grad = None
    for i in range(3):
        weight = jnp.concatenate([w_ref[3 * i + j] for j in range(3)], axis=0)
        term = jnp.dot(
            shifted[(2 - i) * S : (2 - i) * S + CELLS], weight, preferred_element_type=F32
        )
        act_grad = term if act_grad is None else act_grad + term
    out_ref[...] = act_grad


def main_kernel(
    mark_ref, xt_ref, cot_ref, rows_ref, in_stat_ref, affine_ref, act_grad_ref,
    strips_ref, in_ref, keep_ref, send_ref, pre_ref, norm_ref, weight_scr,
):
    def mark(k):
        return mark_ref[k : k + 1] > 0.5

    mean, spread = merge([in_stat_ref[k] for k in range(N_NEAR)], LOCAL * N_FAR)
    rstd = lax.rsqrt(spread * (1.0 / ENTRIES) + EPSILON)
    gain, shift = affine_ref[0:1], affine_ref[1:2]
    norm_ref[...] = jnp.concatenate([mean, rstd], axis=0)

    def affine(raw):
        normed = (raw.astype(F32) - mean) * rstd
        pre = normed * gain + shift
        return normed, pre, 1.0 / (1.0 + jnp.exp(-pre))

    def activated(raw):
        _, pre, sig = affine(raw)
        return (pre * sig).astype(BF16).astype(F32)

    top = jnp.where(mark(FIRST), 0.0, activated(rows_ref[0:S]))
    bottom = jnp.where(mark(LAST), 0.0, activated(rows_ref[S : 2 * S]))
    normed, pre, sig = affine(xt_ref[...])
    own = (pre * sig).astype(BF16).astype(F32)
    windows = jnp.concatenate(beside(jnp.concatenate([top, own, bottom], axis=0)), axis=1)
    grad_out = cot_ref[0]
    for i in range(3):
        part = jnp.dot(grad_out, windows[i * S : i * S + CELLS], preferred_element_type=F32)
        for j in range(3):
            weight_scr[3 * i + j] = part[:, j * C : (j + 1) * C]

    halo = activated(turned(in_ref[0:S], mark(BACK))).astype(BF16)
    halo = jnp.concatenate([halo, halo], axis=0)
    strip = strips_ref[S : 2 * S].astype(F32)
    row = lax.broadcasted_iota(jnp.int32, (S, C), 0)
    first, last = row == 0, row == S - 1
    lines = (
        (jnp.where(last, 0.0, pltpu.roll(strip, S - 1, 0)), jnp.where(first & mark(AT_START), strip, 0.0)),
        (strip, jnp.zeros((S, C), F32)),
        (jnp.where(first, 0.0, pltpu.roll(strip, 1, 0)), jnp.where(last & mark(AT_END), strip, 0.0)),
    )
    terms = [
        lax.dot_general(
            jnp.concatenate(pair, axis=0).astype(BF16),
            halo,
            (((0,), (0,)), ((), ())),
            preferred_element_type=F32,
        )
        for pair in lines
    ]
    for e, taps in enumerate(TAPS):
        for tap, term in zip(taps, terms):
            weight_scr[tap] += jnp.where(mark(SIDE + e), term, 0.0)
    second = mark(CORE)

    def put(row, low, high):
        at = pl.ds(row, N_FAR, stride=CHUNK)
        keep_ref[at, :] = jnp.where(second, high, low)
        send_ref[at, :] = jnp.where(second, low, high)

    for tap in range(9):
        for h in range(2):
            put(
                h * 9 + tap,
                weight_scr[tap, h * 64 : h * 64 + 32],
                weight_scr[tap, h * 64 + 32 : (h + 1) * 64],
            )

    pre_grad = act_grad_ref[...] * (sig * (1.0 + pre * (1.0 - sig)))
    pre_ref[...] = pre_grad
    gain_row = jnp.sum(pre_grad * normed, axis=0, keepdims=True)
    shift_row = jnp.sum(pre_grad, axis=0, keepdims=True)
    normed, pre, sig = affine(strips_ref[0:S])
    more = in_ref[S : 2 * S].astype(F32) * (sig * (1.0 + pre * (1.0 - sig)))
    gain_row = gain_row + jnp.sum(more * normed, axis=0, keepdims=True)
    shift_row = shift_row + jnp.sum(more, axis=0, keepdims=True)
    for k, row in ((18, gain_row), (19, shift_row)):
        row = jnp.broadcast_to(row, (N_FAR, C))
        put(k, row, row)


def end_kernel(
    info_ref, pre_ref, xt_ref, norm_ref, affine_ref, total_ref, pair_ref, others_ref,
    out_ref, gain_sum_ref, shift_sum_ref, side_scr, more_scr,
):
    place = info_ref[0]
    base, odd = place // 2 * 2, place % 2
    for k in range(2):
        at = (odd + k) % 2
        side_scr[base + at] = pair_ref[k]
        side_scr[(base + 2) % 4 + at] = others_ref[k]

    def returned(e, start, size):
        at = pl.ds(pl.multiple_of(start, ROWS), size)
        return side_scr[info_ref[1 + e] % 4, at, :].astype(F32)

    more_scr[...] = jnp.zeros((CELLS, C), F32)
    more_scr[0:S] = jnp.where(place == 0, returned(0, 0, S), 0.0)
    more_scr[CELLS - S : CELLS] = jnp.where(place == 3, returned(2, 0, S), 0.0)
    for e, column in ((3, 0), (1, S - 1)):
        more_scr[pl.ds(column, ROWS, stride=S), :] += returned(e, place * ROWS, ROWS)
    mean, rstd = norm_ref[0:1], norm_ref[1:2]
    gain, shift = affine_ref[0:1], affine_ref[1:2]
    gain_total, shift_total = total_ref[18:19], total_ref[19:20]
    first = group_sum(gain * shift_total) * (1.0 / ENTRIES)
    second = group_sum(gain * gain_total) * (1.0 / ENTRIES)
    normed = (xt_ref[...].astype(F32) - mean) * rstd
    pre = normed * gain + shift
    sig = 1.0 / (1.0 + jnp.exp(-pre))
    pre_grad = pre_ref[...] + more_scr[...] * (sig * (1.0 + pre * (1.0 - sig)))
    out = rstd * (pre_grad * gain - first - normed * second)
    out_ref[0] = out.T.astype(BF16)
    gain_sum_ref[...] = gain_total * SCALE
    shift_sum_ref[...] = shift_total * SCALE


def weight_kernel(whole_ref, out_ref):
    for tap in range(9):
        for h in range(2):
            out_ref[tap, h * 64 : (h + 1) * 64] = (
                whole_ref[pl.ds(h * 9 + tap, 64, stride=CHUNK), :] * SCALE
            )


def sum_kernel(parts, copies, in_ref, out_ref):
    rows = in_ref.shape[0] // parts
    total = in_ref[0:rows]
    for k in range(1, parts):
        total = total + in_ref[k * rows : (k + 1) * rows]
    for k in range(copies):
        out_ref[k * rows : (k + 1) * rows] = total


def add_kernel(mark_ref, own_ref, both_ref, out_ref):
    second = mark_ref[CORE : CORE + 1] > 0.5
    out_ref[...] = own_ref[...] + jnp.where(second, both_ref[0], both_ref[1])


def summed(x, parts, copies):
    rows = x.size // C
    return pl.pallas_call(
        functools.partial(sum_kernel, parts, copies),
        out_shape=shape((rows // parts * copies, C), F32),
        in_specs=[VMEM],
        out_specs=VMEM,
        compiler_params=PARAMS,
    )(x.reshape(rows, C))


def sum_and_pair_kernel(parts, copies, in_ref, own_ref, other_ref, out_ref, pair_ref):
    pair_ref[0] = own_ref[S : 2 * S]
    pair_ref[1] = other_ref[S : 2 * S]
    sum_kernel(parts, copies, in_ref, out_ref)


def exchanged(x, axes, parts):
    x = x.reshape(parts, x.shape[0] // parts // 4, 4, C)
    return lax.all_to_all(x, axes, 0, 0, tiled=True)


def shape(dims, dtype):
    return jax.ShapeDtypeStruct(dims, dtype)


def body(features, cotangent, conv_weight, norm_gain, norm_shift, seam_code, corner_map):
    place = lax.axis_index(SUB).astype(jnp.int32).reshape(1)
    core = lax.axis_index("co").astype(jnp.int32).reshape(1)
    info = jnp.concatenate([place, seam_code[0], corner_map[0], core])
    weight = conv_weight.transpose(1, 0, 2)
    gain, shift = norm_gain.reshape(1, C), norm_shift.reshape(1, C)
    xt, ct, edges, stats = pl.pallas_call(
        start_kernel,
        out_shape=(
            shape((CELLS, C), BF16),
            shape((CELLS, C), BF16),
            shape((2, EDGE, C), BF16),
            shape((N_FAR, 1, C), F32),
        ),
        in_specs=[pl.BlockSpec(memory_space=pltpu.HBM)] * 2,
        out_specs=(VMEM,) * 4,
        scratch_shapes=[pltpu.VMEM((C, CELLS), BF16)] * 2
        + [pltpu.VMEM((CELLS, C), F32)] * 2
        + [pltpu.SemaphoreType.DMA((2, 4))],
        compiler_params=pltpu.CompilerParams(vmem_limit_bytes=START_VMEM),
    )(features, cotangent)
    came = lax.ppermute(edges, "z2", [(0, 1), (1, 0)])
    stats = lax.all_to_all(stats, FAR, 0, 0, tiled=True)
    send, keep, affine, marks = pl.pallas_call(
        middle_kernel,
        out_shape=(
            shape((3, LINE, C), BF16),
            shape((LINE, C), BF16),
            shape((2, C), F32),
            shape((16, C), F32),
        ),
        in_specs=[SMEM] + [VMEM] * 4,
        out_specs=(VMEM,) * 4,
        scratch_shapes=[pltpu.VMEM((2, 4, S, C), BF16)],
        compiler_params=PARAMS,
    )(info, edges, came, gain, shift)
    came = lax.all_gather(send, "z1", axis=0, tiled=False)
    message, strips, rows, stats = pl.pallas_call(
        seam_kernel,
        out_shape=(
            shape((LINE, C), BF16),
            shape((LINE, C), BF16),
            shape((2 * LINE, C), BF16),
            shape((N_NEAR, 1, C), F32),
        ),
        in_specs=[VMEM] * 5,
        out_specs=(VMEM,) * 4,
        compiler_params=PARAMS,
    )(marks, keep, came, stats, weight)
    message = lax.ppermute(
        message,
        tuple(AXES),
        [(4 * t + s, 4 * ((t + STEPS[s]) % 128) + (s + 2) % 4) for t in range(128) for s in range(4)],
    )
    stats = lax.all_to_all(stats, NEAR, 0, 0, tiled=True)
    act_grad = pl.pallas_call(
        grad_kernel,
        out_shape=shape((CELLS, C), F32),
        in_specs=[VMEM] * 3,
        out_specs=VMEM,
        compiler_params=PARAMS,
        cost_estimate=pl.CostEstimate(
            flops=18 * CELLS * C * C, bytes_accessed=10 * CELLS * C, transcendentals=0
        ),
    )(ct, rows, weight)
    parts, send, pre_grad, norm = pl.pallas_call(
        main_kernel,
        out_shape=(
            shape((N_FAR * CHUNK, C), F32),
            shape((N_FAR * CHUNK, C), F32),
            shape((CELLS, C), F32),
            shape((2, C), F32),
        ),
        in_specs=[VMEM] * 9,
        out_specs=(VMEM,) * 4,
        scratch_shapes=[pltpu.VMEM((9, C, C), F32)],
        compiler_params=PARAMS,
    )(marks, xt, cotangent, rows, stats, affine, act_grad, strips, message)
    other = lax.ppermute(message, "z1", [(0, 1), (1, 0)])
    both = lax.all_gather(send, "co", axis=0, tiled=False)
    parts = pl.pallas_call(
        add_kernel,
        out_shape=shape((N_FAR * CHUNK, C), F32),
        in_specs=[VMEM] * 3,
        out_specs=VMEM,
        compiler_params=PARAMS,
    )(marks, parts, both)
    parts, pair = pl.pallas_call(
        functools.partial(sum_and_pair_kernel, N_FAR, 8),
        out_shape=(shape((8 * CHUNK, C), F32), shape((2, S, C), BF16)),
        in_specs=[VMEM] * 3,
        out_specs=(VMEM,) * 2,
        compiler_params=PARAMS,
    )(exchanged(parts, FAR, N_FAR).reshape(N_FAR * CHUNK, C), message, other)
    others = lax.ppermute(pair, "z2", [(0, 1), (1, 0)])
    parts = summed(exchanged(parts, ("zh", "z2", "z1"), 8), 8, N_FAR)
    half = exchanged(parts, FAR, N_FAR)
    whole = lax.all_gather(half, "co", axis=0, tiled=True)
    grad_input, grad_gain, grad_shift = pl.pallas_call(
        end_kernel,
        out_shape=(shape((1, C, CELLS), BF16), shape((1, C), F32), shape((1, C), F32)),
        in_specs=[SMEM] + [VMEM] * 7,
        out_specs=(VMEM,) * 3,
        scratch_shapes=[pltpu.VMEM((4, S, C), BF16), pltpu.VMEM((CELLS, C), F32)],
        compiler_params=PARAMS,
    )(info, pre_grad, xt, norm, affine, parts, pair, others)
    grad_weight = pl.pallas_call(
        weight_kernel,
        out_shape=shape((9, C, C), F32),
        in_specs=[VMEM],
        out_specs=VMEM,
        compiler_params=PARAMS,
    )(whole.reshape(64 * CHUNK, C)).transpose(1, 0, 2)
    return grad_input, grad_weight, grad_gain.reshape(C), grad_shift.reshape(C)


def solution(mesh):
    fine = Mesh(mesh.devices.reshape(tuple(AXES.values())), tuple(AXES))
    return jax.shard_map(
        body,
        mesh=fine,
        in_specs=(
            P(TILE, None, SUB),
            P(TILE, None, SUB),
            P(),
            P(),
            P(),
            P(TILE, None),
            P(TILE, None),
        ),
        out_specs=(P(TILE, None, SUB), P(), P(), P()),
        check_vma=False,
    )
```

```python
import functools
import math

import jax
import jax.numpy as jnp
from jax import lax
from jax.experimental import pallas as pl
from jax.experimental.pallas import tpu as pltpu
from jax.sharding import Mesh
from jax.sharding import PartitionSpec as P

GC = 4
S = 64
PER_GROUP = 8
EPSILON = 1e-05
STEPS = (-GC, 1, GC, -1)
ROWS = 16
CELLS = ROWS * S
C = 128
LINE = 2 * S
EDGE = 2 * S + 2 * ROWS
CHUNK = 20

TILE = ("y", "x", "zh", "co")
AXES = {"y": 8, "x": 4, "zh": 2, "co": 2, "z2": 2, "z1": 2}
SUB = ("z2", "z1")
NEAR = ("zh", "co", "z2", "z1")
FAR = ("y", "x")
N_NEAR = 16
N_FAR = 32
DEVICES = 512
ENTRIES = DEVICES * CELLS * PER_GROUP
LOCAL = CELLS * PER_GROUP
SCALE = 1.0 / math.sqrt(DEVICES * CELLS)

F32 = jnp.float32
BF16 = jnp.bfloat16
VMEM = pl.BlockSpec(memory_space=pltpu.VMEM)
SMEM = pl.BlockSpec(memory_space=pltpu.SMEM)
START_VMEM = 56360960
PARAMS = pltpu.CompilerParams(vmem_limit_bytes=40 * 1024 * 1024)


def group_sum(row):
    total = jnp.broadcast_to(row, (8, C))
    lane = lax.broadcasted_iota(jnp.int32, (8, C), 1)
    for by in (1, 2, 4):
        other = jnp.where(
            (lane & by) != 0, pltpu.roll(total, by, 1), pltpu.roll(total, C - by, 1)
        )
        total = total + other
    return total[0:1]


def packed(mean, spread):
    lane = lax.broadcasted_iota(jnp.int32, (1, C), 1)
    return jnp.where(lane % 2 == 0, mean, spread)


def unpacked(row):
    row = jnp.broadcast_to(row, (8, C))
    even = lax.broadcasted_iota(jnp.int32, (8, C), 1) % 2 == 0
    mean = jnp.where(even, row, pltpu.roll(row, 1, 1))
    spread = jnp.where(even, pltpu.roll(row, C - 1, 1), row)
    return mean[0:1], spread[0:1]


def merge(rows, count):
    means, squares = zip(*[unpacked(row) for row in rows])
    mean = sum(means) * (1.0 / len(means))
    spread = sum(squares) + float(count) * sum((m - mean) * (m - mean) for m in means)
    return mean, spread


def edge_picker():
    row = lax.broadcasted_iota(jnp.int32, (EDGE, CELLS), 0)
    cell = lax.broadcasted_iota(jnp.int32, (EDGE, CELLS), 1)
    wanted = jnp.where(row < S, row, row + CELLS - 2 * S)
    wanted = jnp.where(row >= 2 * S, (row - 2 * S) * S + S - 1, wanted)
    wanted = jnp.where(row >= 2 * S + ROWS, (row - 2 * S - ROWS) * S, wanted)
    return jnp.where(cell == wanted, 1.0, 0.0).astype(BF16)


def start_kernel(x_hbm, c_hbm, edge_ref, stat_ref, x_in, c_in, sems):
    copies = []
    for kind, (far, near) in enumerate(((x_hbm, x_in), (c_hbm, c_in))):
        for k in range(4):
            at = pl.ds(k * 32, 32)
            copies.append(pltpu.make_async_copy(far.at[0, at], near.at[at], sems.at[kind, k]))
            copies[-1].start()
    picker = edge_picker()
    for copy in copies[:4]:
        copy.wait()
    x = x_in[...].astype(F32)
    blocks = [x[:, k * C : (k + 1) * C] for k in range(CELLS // C)]

    def channel_sums(parts):
        return group_sum(jnp.sum(sum(parts).T, axis=0, keepdims=True))

    mean = channel_sums(blocks) * (1.0 / LOCAL)
    column = jnp.broadcast_to(mean, (C, C)).T
    spread = channel_sums([(v - column) * (v - column) for v in blocks])
    stat_ref[...] = jnp.broadcast_to(packed(mean, spread)[None], (N_FAR, 1, C))
    for copy in copies[4:]:
        copy.wait()
    for kind, ref in enumerate((x_in, c_in)):
        edge_ref[kind] = lax.dot_general(
            picker, ref[...], (((1,), (1,)), ((), ())), preferred_element_type=F32
        ).astype(BF16)


def corners_of(info_ref, side):
    start = jnp.where(side == 1, 1, jnp.where(side == 2, 3, 0))
    end = jnp.where(side == 0, 1, jnp.where(side == 3, 3, 2))
    return info_ref[5 + start] == side % 2, info_ref[5 + end] == side % 2


TAPS = ((0, 1, 2), (2, 5, 8), (6, 7, 8), (0, 3, 6))
FIRST, LAST, CORE, SIDE, AT_START, AT_END, BACK, ODD = 0, 1, 2, 3, 7, 8, 9, 10


def middle_kernel(
    info_ref, own_ref, other_ref, gain_ref, shift_ref,
    send_ref, left_ref, affine_ref, mark_ref, side_scr,
):
    place = info_ref[0]
    odd = place % 2
    pair = (place + 2) % 4
    affine_ref[0:1], affine_ref[1:2] = gain_ref[...], shift_ref[...]
    mine = side_facing(info_ref, place)
    at_start, at_end = corners_of(info_ref, mine)
    marks = (
        [place == 0, place == 3, info_ref[9] == 1]
        + [mine == e for e in range(4)]
        + [at_start, at_end, info_ref[1 + mine] // 4 == 1, odd == 1]
    )
    for k, mark in enumerate(marks):
        mark_ref[k : k + 1] = jnp.full((1, C), jnp.where(mark, 1.0, 0.0), F32)
    zero = jnp.zeros((S, C), BF16)
    first, last = slice(0, S), slice(S, 2 * S)
    for kind in range(2):
        side_scr[kind, 0] = jnp.where(
            place == 0, own_ref[kind, first], jnp.where(pair == 0, other_ref[kind, first], zero)
        )
        side_scr[kind, 2] = jnp.where(
            place == 3, own_ref[kind, last], jnp.where(pair == 3, other_ref[kind, last], zero)
        )
        for k, side in enumerate((1, 3)):
            at = slice(2 * S + k * ROWS, 2 * S + (k + 1) * ROWS)
            side_scr[kind, side] = zero
            for who, ref in ((place, own_ref), (pair, other_ref)):
                rows = pl.ds(pl.multiple_of(who * ROWS, ROWS), ROWS)
                side_scr[kind, side, rows, :] = ref[kind, at]
        here = slice(kind * S, (kind + 1) * S)
        send_ref[0, here] = side_scr[kind, side_facing(info_ref, place + 1 - 2 * odd)]
        left_ref[here] = side_scr[kind, side_facing(info_ref, place)]
        send_ref[1, here] = jnp.where(odd == 1, own_ref[kind, first], own_ref[kind, last])
        send_ref[2, here] = jnp.where(place == 0, other_ref[kind, first], other_ref[kind, last])


def side_facing(info_ref, direction):
    side = jnp.int32(0)
    for e in range(1, 4):
        side = jnp.where(info_ref[1 + e] % 4 == direction, e, side)
    return side


def flip_matrix():
    a = lax.broadcasted_iota(jnp.int32, (S, S), 0)
    b = lax.broadcasted_iota(jnp.int32, (S, S), 1)
    return jnp.where(a + b == S - 1, 1.0, 0.0).astype(BF16)


def turned(strip, flag):
    back = jnp.dot(flip_matrix(), strip, preferred_element_type=F32)
    return jnp.where(flag, back, strip.astype(F32)).astype(BF16)


def seam_kernel(
    mark_ref, keep_ref, in_ref, in_stat_ref, w_ref, message_ref, strips_ref, rows_ref, stat_ref,
):
    def mark(k):
        return mark_ref[k : k + 1] > 0.5

    def other(k):
        return jnp.where(mark(ODD), in_ref[0, k].astype(F32), in_ref[1, k].astype(F32))

    strips = (keep_ref[...].astype(F32) + other(0)).astype(BF16)
    strips_ref[...] = strips
    grads = strips[S : 2 * S]
    parts = []
    for k in range(3):
        weight = w_ref[TAPS[0][k]].astype(F32)
        for e in range(1, 4):
            weight = jnp.where(mark(SIDE + e), w_ref[TAPS[e][k]].astype(F32), weight)
        parts.append(jnp.dot(grads, weight.astype(BF16), preferred_element_type=F32))
    row = lax.broadcasted_iota(jnp.int32, (S, C), 0)
    first, last = row == 0, row == S - 1
    grad = parts[1]
    grad = grad + jnp.where(last, 0.0, pltpu.roll(parts[0], S - 1, 0))
    grad = grad + jnp.where(first, 0.0, pltpu.roll(parts[2], 1, 0))
    grad = grad + jnp.where(first & mark(AT_START), parts[0], 0.0)
    grad = grad + jnp.where(last & mark(AT_END), parts[2], 0.0)
    message_ref[0:S] = strips[0:S]
    message_ref[S : 2 * S] = turned(grad.astype(BF16), mark(BACK))
    direct, passed = other(1), other(2)
    above = jnp.where(mark(ODD), direct, passed)
    below = jnp.where(mark(ODD), passed, direct)
    rows_ref[0:S] = above[0:S].astype(BF16)
    rows_ref[S : 2 * S] = below[0:S].astype(BF16)
    rows_ref[2 * S : 3 * S] = jnp.where(mark(FIRST), 0.0, above[S : 2 * S]).astype(BF16)
    rows_ref[3 * S : 4 * S] = jnp.where(mark(LAST), 0.0, below[S : 2 * S]).astype(BF16)
    stats = packed(*merge([in_stat_ref[k] for k in range(N_FAR)], LOCAL))
    stat_ref[...] = jnp.broadcast_to(stats[None], (N_NEAR, 1, C))


def beside(middle):
    wide = middle.shape[0]
    column = lax.broadcasted_iota(jnp.int32, middle.shape, 0) & (S - 1)
    before = jnp.where(column == 0, 0.0, pltpu.roll(middle, 1, 0))
    after = jnp.where(column == S - 1, 0.0, pltpu.roll(middle, wide - 1, 0))
    return before.astype(BF16), middle.astype(BF16), after.astype(BF16)


def grad_kernel(x_ref, c_ref, rows_ref, w_ref, out_ref, xt_ref):
    xt_ref[...] = x_ref[0].astype(F32).T.astype(BF16)
    above, below = rows_ref[2 * S : 3 * S].astype(F32), rows_ref[3 * S : 4 * S].astype(F32)
    grads = jnp.concatenate([above, c_ref[0].astype(F32).T, below], axis=0)
    shifted = jnp.concatenate(beside(grads)[::-1], axis=1)
    act_grad = None
    for i in range(3):
        weight = jnp.concatenate([w_ref[3 * i + j] for j in range(3)], axis=0)
        term = jnp.dot(
            shifted[(2 - i) * S : (2 - i) * S + CELLS], weight, preferred_element_type=F32
        )
        act_grad = term if act_grad is None else act_grad + term
    out_ref[...] = act_grad


def main_kernel(
    mark_ref, xt_ref, cot_ref, rows_ref, in_stat_ref, affine_ref, act_grad_ref,
    strips_ref, in_ref, keep_ref, send_ref, pre_ref, norm_ref, weight_scr,
):
    def mark(k):
        return mark_ref[k : k + 1] > 0.5

    mean, spread = merge([in_stat_ref[k] for k in range(N_NEAR)], LOCAL * N_FAR)
    rstd = lax.rsqrt(spread * (1.0 / ENTRIES) + EPSILON)
    gain, shift = affine_ref[0:1], affine_ref[1:2]
    norm_ref[...] = jnp.concatenate([mean, rstd], axis=0)

    def affine(raw):
        normed = (raw.astype(F32) - mean) * rstd
        pre = normed * gain + shift
        return normed, pre, 1.0 / (1.0 + jnp.exp(-pre))

    def activated(raw):
        _, pre, sig = affine(raw)
        return (pre * sig).astype(BF16).astype(F32)

    top = jnp.where(mark(FIRST), 0.0, activated(rows_ref[0:S]))
    bottom = jnp.where(mark(LAST), 0.0, activated(rows_ref[S : 2 * S]))
    normed, pre, sig = affine(xt_ref[...])
    own = (pre * sig).astype(BF16).astype(F32)
    windows = jnp.concatenate(beside(jnp.concatenate([top, own, bottom], axis=0)), axis=1)
    grad_out = cot_ref[0]
    for i in range(3):
        part = jnp.dot(grad_out, windows[i * S : i * S + CELLS], preferred_element_type=F32)
        for j in range(3):
            weight_scr[3 * i + j] = part[:, j * C : (j + 1) * C]

    halo = activated(turned(in_ref[0:S], mark(BACK))).astype(BF16)
    halo = jnp.concatenate([halo, halo], axis=0)
    strip = strips_ref[S : 2 * S].astype(F32)
    row = lax.broadcasted_iota(jnp.int32, (S, C), 0)
    first, last = row == 0, row == S - 1
    lines = (
        (jnp.where(last, 0.0, pltpu.roll(strip, S - 1, 0)), jnp.where(first & mark(AT_START), strip, 0.0)),
        (strip, jnp.zeros((S, C), F32)),
        (jnp.where(first, 0.0, pltpu.roll(strip, 1, 0)), jnp.where(last & mark(AT_END), strip, 0.0)),
    )
    terms = [
        lax.dot_general(
            jnp.concatenate(pair, axis=0).astype(BF16),
            halo,
            (((0,), (0,)), ((), ())),
            preferred_element_type=F32,
        )
        for pair in lines
    ]
    for e, taps in enumerate(TAPS):
        for tap, term in zip(taps, terms):
            weight_scr[tap] += jnp.where(mark(SIDE + e), term, 0.0)
    second = mark(CORE)

    def put(row, low, high):
        at = pl.ds(row, N_FAR, stride=CHUNK)
        keep_ref[at, :] = jnp.where(second, high, low)
        send_ref[at, :] = jnp.where(second, low, high)

    for tap in range(9):
        for h in range(2):
            put(
                h * 9 + tap,
                weight_scr[tap, h * 64 : h * 64 + 32],
                weight_scr[tap, h * 64 + 32 : (h + 1) * 64],
            )

    pre_grad = act_grad_ref[...] * (sig * (1.0 + pre * (1.0 - sig)))
    pre_ref[...] = pre_grad
    gain_row = jnp.sum(pre_grad * normed, axis=0, keepdims=True)
    shift_row = jnp.sum(pre_grad, axis=0, keepdims=True)
    normed, pre, sig = affine(strips_ref[0:S])
    more = in_ref[S : 2 * S].astype(F32) * (sig * (1.0 + pre * (1.0 - sig)))
    gain_row = gain_row + jnp.sum(more * normed, axis=0, keepdims=True)
    shift_row = shift_row + jnp.sum(more, axis=0, keepdims=True)
    for k, row in ((18, gain_row), (19, shift_row)):
        row = jnp.broadcast_to(row, (N_FAR, C))
        put(k, row, row)


def slope_kernel(xt_ref, norm_ref, affine_ref, out_ref):
    normed = (xt_ref[...].astype(F32) - norm_ref[0:1]) * norm_ref[1:2]
    pre = normed * affine_ref[0:1] + affine_ref[1:2]
    sig = 1.0 / (1.0 + jnp.exp(-pre))
    out_ref[...] = sig * (1.0 + pre * (1.0 - sig))


def end_kernel(
    info_ref, pre_ref, xt_ref, norm_ref, affine_ref, total_ref, in_ref, slope_ref,
    out_ref, gain_sum_ref, shift_sum_ref, side_scr, more_scr,
):
    place = info_ref[0]
    odd = place % 2
    for half in range(2):
        for k in range(2):
            side_scr[2 * half + (odd + k) % 2] = in_ref[half, k]

    def returned(e, start, size):
        at = pl.ds(pl.multiple_of(start, ROWS), size)
        return side_scr[info_ref[1 + e] % 4, at, :].astype(F32)

    more_scr[...] = jnp.zeros((CELLS, C), F32)
    more_scr[0:S] = jnp.where(place == 0, returned(0, 0, S), 0.0)
    more_scr[CELLS - S : CELLS] = jnp.where(place == 3, returned(2, 0, S), 0.0)
    for e, column in ((3, 0), (1, S - 1)):
        more_scr[pl.ds(column, ROWS, stride=S), :] += returned(e, place * ROWS, ROWS)
    mean, rstd = norm_ref[0:1], norm_ref[1:2]
    gain = affine_ref[0:1]
    gain_total, shift_total = total_ref[0:1], total_ref[1:2]
    first = group_sum(gain * shift_total) * (1.0 / ENTRIES)
    second = group_sum(gain * gain_total) * (1.0 / ENTRIES)
    normed = (xt_ref[...].astype(F32) - mean) * rstd
    pre_grad = pre_ref[...] + more_scr[...] * slope_ref[...]
    out = rstd * (pre_grad * gain - first - normed * second)
    out_ref[0] = out.T.astype(BF16)
    gain_sum_ref[...] = gain_total * SCALE
    shift_sum_ref[...] = shift_total * SCALE


def weight_kernel(whole_ref, out_ref):
    for tap in range(9):
        for h in range(2):
            out_ref[tap, h * 64 : (h + 1) * 64] = (
                whole_ref[pl.ds(h * 9 + tap, 64, stride=CHUNK), :] * SCALE
            )


def sum_kernel(parts, copies, in_ref, out_ref):
    rows = in_ref.shape[0] // parts
    total = in_ref[0:rows]
    for k in range(1, parts):
        total = total + in_ref[k * rows : (k + 1) * rows]
    for k in range(copies):
        out_ref[k * rows : (k + 1) * rows] = total


def last_sum_kernel(in_ref, out_ref, sums_ref):
    sum_kernel(8, N_FAR, in_ref, out_ref)
    sums_ref[...] = out_ref[18:20]


def add_kernel(mark_ref, own_ref, both_ref, out_ref):
    second = mark_ref[CORE : CORE + 1] > 0.5
    out_ref[...] = own_ref[...] + jnp.where(second, both_ref[0], both_ref[1])


def sum_and_pair_kernel(parts, copies, in_ref, own_ref, other_ref, _, out_ref, pair_ref):
    pair_ref[0] = own_ref[S : 2 * S]
    pair_ref[1] = other_ref[S : 2 * S]
    sum_kernel(parts, copies, in_ref, out_ref)


def exchanged(x, axes, parts):
    x = x.reshape(parts, x.shape[0] // parts // 4, 4, C)
    return lax.all_to_all(x, axes, 0, 0, tiled=True)


def shape(dims, dtype):
    return jax.ShapeDtypeStruct(dims, dtype)


def body(features, cotangent, conv_weight, norm_gain, norm_shift, seam_code, corner_map):
    place = lax.axis_index(SUB).astype(jnp.int32).reshape(1)
    core = lax.axis_index("co").astype(jnp.int32).reshape(1)
    info = jnp.concatenate([place, seam_code[0], corner_map[0], core])
    weight = conv_weight.transpose(1, 0, 2)
    gain, shift = norm_gain.reshape(1, C), norm_shift.reshape(1, C)
    edges, stats = pl.pallas_call(
        start_kernel,
        out_shape=(shape((2, EDGE, C), BF16), shape((N_FAR, 1, C), F32)),
        in_specs=[pl.BlockSpec(memory_space=pltpu.HBM)] * 2,
        out_specs=(VMEM,) * 2,
        scratch_shapes=[pltpu.VMEM((C, CELLS), BF16)] * 2 + [pltpu.SemaphoreType.DMA((2, 4))],
        compiler_params=pltpu.CompilerParams(vmem_limit_bytes=START_VMEM),
    )(features, cotangent)
    came = lax.ppermute(edges, "z2", [(0, 1), (1, 0)])
    stats = lax.all_to_all(stats, FAR, 0, 0, tiled=True)
    send, keep, affine, marks = pl.pallas_call(
        middle_kernel,
        out_shape=(
            shape((3, LINE, C), BF16),
            shape((LINE, C), BF16),
            shape((2, C), F32),
            shape((16, C), F32),
        ),
        in_specs=[SMEM] + [VMEM] * 4,
        out_specs=(VMEM,) * 4,
        scratch_shapes=[pltpu.VMEM((2, 4, S, C), BF16)],
        compiler_params=PARAMS,
    )(info, edges, came, gain, shift)
    came = lax.all_gather(send, "z1", axis=0, tiled=False)
    message, strips, rows, stats = pl.pallas_call(
        seam_kernel,
        out_shape=(
            shape((LINE, C), BF16),
            shape((LINE, C), BF16),
            shape((2 * LINE, C), BF16),
            shape((N_NEAR, 1, C), F32),
        ),
        in_specs=[VMEM] * 5,
        out_specs=(VMEM,) * 4,
        compiler_params=PARAMS,
    )(marks, keep, came, stats, weight)
    message = lax.ppermute(
        message,
        tuple(AXES),
        [(4 * t + s, 4 * ((t + STEPS[s]) % 128) + (s + 2) % 4) for t in range(128) for s in range(4)],
    )
    stats = lax.all_to_all(stats, NEAR, 0, 0, tiled=True)
    act_grad, xt = pl.pallas_call(
        grad_kernel,
        out_shape=(shape((CELLS, C), F32), shape((CELLS, C), BF16)),
        in_specs=[VMEM] * 4,
        out_specs=(VMEM,) * 2,
        compiler_params=PARAMS,
        cost_estimate=pl.CostEstimate(
            flops=18 * CELLS * C * C, bytes_accessed=10 * CELLS * C, transcendentals=0
        ),
    )(features, cotangent, rows, weight)
    parts, send, pre_grad, norm = pl.pallas_call(
        main_kernel,
        out_shape=(
            shape((N_FAR * CHUNK, C), F32),
            shape((N_FAR * CHUNK, C), F32),
            shape((CELLS, C), F32),
            shape((2, C), F32),
        ),
        in_specs=[VMEM] * 9,
        out_specs=(VMEM,) * 4,
        scratch_shapes=[pltpu.VMEM((9, C, C), F32)],
        compiler_params=PARAMS,
    )(marks, xt, cotangent, rows, stats, affine, act_grad, strips, message)
    slope = pl.pallas_call(
        slope_kernel,
        out_shape=shape((CELLS, C), F32),
        in_specs=[VMEM] * 3,
        out_specs=VMEM,
        compiler_params=PARAMS,
    )(xt, norm, affine)
    other = lax.ppermute(message, "z1", [(0, 1), (1, 0)])
    both = lax.all_gather(send, "co", axis=0, tiled=False)
    parts = pl.pallas_call(
        add_kernel,
        out_shape=shape((N_FAR * CHUNK, C), F32),
        in_specs=[VMEM] * 3,
        out_specs=VMEM,
        compiler_params=PARAMS,
    )(marks, parts, both)
    parts, pair = pl.pallas_call(
        functools.partial(sum_and_pair_kernel, N_FAR, 8),
        out_shape=(shape((8 * CHUNK, C), F32), shape((2, S, C), BF16)),
        in_specs=[VMEM] * 4,
        out_specs=(VMEM,) * 2,
        compiler_params=PARAMS,
    )(exchanged(parts, FAR, N_FAR).reshape(N_FAR * CHUNK, C), message, other, slope)
    sides = lax.all_gather(pair, "z2", axis=0, tiled=False)
    parts, sums = pl.pallas_call(
        last_sum_kernel,
        out_shape=(shape((N_FAR * CHUNK, C), F32), shape((2, C), F32)),
        in_specs=[VMEM],
        out_specs=(VMEM,) * 2,
        compiler_params=PARAMS,
    )(exchanged(parts, ("zh", "z2", "z1"), 8).reshape(8 * CHUNK, C))
    half = exchanged(parts, FAR, N_FAR)
    whole = lax.all_gather(half, "co", axis=0, tiled=True)
    grad_input, grad_gain, grad_shift = pl.pallas_call(
        end_kernel,
        out_shape=(shape((1, C, CELLS), BF16), shape((1, C), F32), shape((1, C), F32)),
        in_specs=[SMEM] + [VMEM] * 7,
        out_specs=(VMEM,) * 3,
        scratch_shapes=[pltpu.VMEM((4, S, C), BF16), pltpu.VMEM((CELLS, C), F32)],
        compiler_params=PARAMS,
    )(info, pre_grad, xt, norm, affine, sums, sides, slope)
    grad_weight = pl.pallas_call(
        weight_kernel,
        out_shape=shape((9, C, C), F32),
        in_specs=[VMEM],
        out_specs=VMEM,
        compiler_params=PARAMS,
    )(whole.reshape(64 * CHUNK, C)).transpose(1, 0, 2)
    return grad_input, grad_weight, grad_gain.reshape(C), grad_shift.reshape(C)


def solution(mesh):
    fine = Mesh(mesh.devices.reshape(tuple(AXES.values())), tuple(AXES))
    return jax.shard_map(
        body,
        mesh=fine,
        in_specs=(
            P(TILE, None, SUB),
            P(TILE, None, SUB),
            P(),
            P(),
            P(),
            P(TILE, None),
            P(TILE, None),
        ),
        out_specs=(P(TILE, None, SUB), P(), P(), P()),
        check_vma=False,
    )
```

```python
import functools
import math

import jax
import jax.numpy as jnp
from jax import lax
from jax.experimental import pallas as pl
from jax.experimental.pallas import tpu as pltpu
from jax.sharding import Mesh
from jax.sharding import PartitionSpec as P

GC = 4
S = 64
PER_GROUP = 8
EPSILON = 1e-05
STEPS = (-GC, 1, GC, -1)
ROWS = 16
CELLS = ROWS * S
C = 128
LINE = 2 * S
EDGE = 2 * S + 2 * ROWS
CHUNK = 20
TAPPED = 18

TILE = ("y", "x", "zh", "co")
AXES = {"y": 8, "x": 4, "zh": 2, "co": 2, "z2": 2, "z1": 2}
SUB = ("z2", "z1")
NEAR = ("zh", "co", "z2", "z1")
FAR = ("y", "x")
N_NEAR = 16
N_FAR = 32
DEVICES = 512
ENTRIES = DEVICES * CELLS * PER_GROUP
LOCAL = CELLS * PER_GROUP
SCALE = 1.0 / math.sqrt(DEVICES * CELLS)

F32 = jnp.float32
BF16 = jnp.bfloat16
VMEM = pl.BlockSpec(memory_space=pltpu.VMEM)
SMEM = pl.BlockSpec(memory_space=pltpu.SMEM)
START_VMEM = 56360960
PARAMS = pltpu.CompilerParams(vmem_limit_bytes=40 * 1024 * 1024)


def group_sum(row):
    total = jnp.broadcast_to(row, (8, C))
    lane = lax.broadcasted_iota(jnp.int32, (8, C), 1)
    for by in (1, 2, 4):
        other = jnp.where(
            (lane & by) != 0, pltpu.roll(total, by, 1), pltpu.roll(total, C - by, 1)
        )
        total = total + other
    return total[0:1]


def packed(mean, spread):
    lane = lax.broadcasted_iota(jnp.int32, (1, C), 1)
    return jnp.where(lane % 2 == 0, mean, spread)


def unpacked(row):
    row = jnp.broadcast_to(row, (8, C))
    even = lax.broadcasted_iota(jnp.int32, (8, C), 1) % 2 == 0
    mean = jnp.where(even, row, pltpu.roll(row, 1, 1))
    spread = jnp.where(even, pltpu.roll(row, C - 1, 1), row)
    return mean[0:1], spread[0:1]


def merge(rows, count):
    means, squares = zip(*[unpacked(row) for row in rows])
    mean = sum(means) * (1.0 / len(means))
    spread = sum(squares) + float(count) * sum((m - mean) * (m - mean) for m in means)
    return mean, spread


def edge_picker():
    row = lax.broadcasted_iota(jnp.int32, (EDGE, CELLS), 0)
    cell = lax.broadcasted_iota(jnp.int32, (EDGE, CELLS), 1)
    wanted = jnp.where(row < S, row, row + CELLS - 2 * S)
    wanted = jnp.where(row >= 2 * S, (row - 2 * S) * S + S - 1, wanted)
    wanted = jnp.where(row >= 2 * S + ROWS, (row - 2 * S - ROWS) * S, wanted)
    return jnp.where(cell == wanted, 1.0, 0.0).astype(BF16)


def start_kernel(x_hbm, c_hbm, edge_ref, stat_ref, x_in, c_in, sems):
    copies = []
    for kind, (far, near) in enumerate(((x_hbm, x_in), (c_hbm, c_in))):
        for k in range(4):
            at = pl.ds(k * 32, 32)
            copies.append(pltpu.make_async_copy(far.at[0, at], near.at[at], sems.at[kind, k]))
            copies[-1].start()
    picker = edge_picker()
    for copy in copies[:4]:
        copy.wait()
    x = x_in[...].astype(F32)
    blocks = [x[:, k * C : (k + 1) * C] for k in range(CELLS // C)]

    def channel_sums(parts):
        return group_sum(jnp.sum(sum(parts).T, axis=0, keepdims=True))

    mean = channel_sums(blocks) * (1.0 / LOCAL)
    column = jnp.broadcast_to(mean, (C, C)).T
    spread = channel_sums([(v - column) * (v - column) for v in blocks])
    stat_ref[...] = jnp.broadcast_to(packed(mean, spread)[None], (N_FAR, 1, C))
    for copy in copies[4:]:
        copy.wait()
    for kind, ref in enumerate((x_in, c_in)):
        edge_ref[kind] = lax.dot_general(
            picker, ref[...], (((1,), (1,)), ((), ())), preferred_element_type=F32
        ).astype(BF16)


def corners_of(info_ref, side):
    start = jnp.where(side == 1, 1, jnp.where(side == 2, 3, 0))
    end = jnp.where(side == 0, 1, jnp.where(side == 3, 3, 2))
    return info_ref[5 + start] == side % 2, info_ref[5 + end] == side % 2


TAPS = ((0, 1, 2), (2, 5, 8), (6, 7, 8), (0, 3, 6))
FIRST, LAST, CORE, SIDE, AT_START, AT_END, BACK, ODD = 0, 1, 2, 3, 7, 8, 9, 10


def middle_kernel(
    info_ref, own_ref, other_ref, gain_ref, shift_ref,
    send_ref, left_ref, affine_ref, mark_ref, side_scr,
):
    place = info_ref[0]
    odd = place % 2
    pair = (place + 2) % 4
    affine_ref[0:1], affine_ref[1:2] = gain_ref[...], shift_ref[...]
    mine = side_facing(info_ref, place)
    at_start, at_end = corners_of(info_ref, mine)
    marks = (
        [place == 0, place == 3, info_ref[9] == 1]
        + [mine == e for e in range(4)]
        + [at_start, at_end, info_ref[1 + mine] // 4 == 1, odd == 1]
    )
    for k, mark in enumerate(marks):
        mark_ref[k : k + 1] = jnp.full((1, C), jnp.where(mark, 1.0, 0.0), F32)
    zero = jnp.zeros((S, C), BF16)
    first, last = slice(0, S), slice(S, 2 * S)
    for kind in range(2):
        side_scr[kind, 0] = jnp.where(
            place == 0, own_ref[kind, first], jnp.where(pair == 0, other_ref[kind, first], zero)
        )
        side_scr[kind, 2] = jnp.where(
            place == 3, own_ref[kind, last], jnp.where(pair == 3, other_ref[kind, last], zero)
        )
        for k, side in enumerate((1, 3)):
            at = slice(2 * S + k * ROWS, 2 * S + (k + 1) * ROWS)
            side_scr[kind, side] = zero
            for who, ref in ((place, own_ref), (pair, other_ref)):
                rows = pl.ds(pl.multiple_of(who * ROWS, ROWS), ROWS)
                side_scr[kind, side, rows, :] = ref[kind, at]
        here = slice(kind * S, (kind + 1) * S)
        send_ref[0, here] = side_scr[kind, side_facing(info_ref, place + 1 - 2 * odd)]
        left_ref[here] = side_scr[kind, side_facing(info_ref, place)]
        send_ref[1, here] = jnp.where(odd == 1, own_ref[kind, first], own_ref[kind, last])
        send_ref[2, here] = jnp.where(place == 0, other_ref[kind, first], other_ref[kind, last])


def side_facing(info_ref, direction):
    side = jnp.int32(0)
    for e in range(1, 4):
        side = jnp.where(info_ref[1 + e] % 4 == direction, e, side)
    return side


def flip_matrix():
    a = lax.broadcasted_iota(jnp.int32, (S, S), 0)
    b = lax.broadcasted_iota(jnp.int32, (S, S), 1)
    return jnp.where(a + b == S - 1, 1.0, 0.0).astype(BF16)


def turned(strip, flag):
    back = jnp.dot(flip_matrix(), strip, preferred_element_type=F32)
    return jnp.where(flag, back, strip.astype(F32)).astype(BF16)


def seam_kernel(
    mark_ref, keep_ref, in_ref, in_stat_ref, w_ref, message_ref, strips_ref, rows_ref, stat_ref,
):
    def mark(k):
        return mark_ref[k : k + 1] > 0.5

    def other(k):
        return jnp.where(mark(ODD), in_ref[0, k].astype(F32), in_ref[1, k].astype(F32))

    strips = (keep_ref[...].astype(F32) + other(0)).astype(BF16)
    strips_ref[...] = strips
    grads = strips[S : 2 * S]
    parts = []
    for k in range(3):
        weight = w_ref[TAPS[0][k]].astype(F32)
        for e in range(1, 4):
            weight = jnp.where(mark(SIDE + e), w_ref[TAPS[e][k]].astype(F32), weight)
        parts.append(jnp.dot(grads, weight.astype(BF16), preferred_element_type=F32))
    row = lax.broadcasted_iota(jnp.int32, (S, C), 0)
    first, last = row == 0, row == S - 1
    grad = parts[1]
    grad = grad + jnp.where(last, 0.0, pltpu.roll(parts[0], S - 1, 0))
    grad = grad + jnp.where(first, 0.0, pltpu.roll(parts[2], 1, 0))
    grad = grad + jnp.where(first & mark(AT_START), parts[0], 0.0)
    grad = grad + jnp.where(last & mark(AT_END), parts[2], 0.0)
    message_ref[0:S] = strips[0:S]
    message_ref[S : 2 * S] = turned(grad.astype(BF16), mark(BACK))
    direct, passed = other(1), other(2)
    above = jnp.where(mark(ODD), direct, passed)
    below = jnp.where(mark(ODD), passed, direct)
    rows_ref[0:S] = above[0:S].astype(BF16)
    rows_ref[S : 2 * S] = below[0:S].astype(BF16)
    rows_ref[2 * S : 3 * S] = jnp.where(mark(FIRST), 0.0, above[S : 2 * S]).astype(BF16)
    rows_ref[3 * S : 4 * S] = jnp.where(mark(LAST), 0.0, below[S : 2 * S]).astype(BF16)
    stats = packed(*merge([in_stat_ref[k] for k in range(N_FAR)], LOCAL))
    stat_ref[...] = jnp.broadcast_to(stats[None], (N_NEAR, 1, C))


def beside(middle):
    wide = middle.shape[0]
    column = lax.broadcasted_iota(jnp.int32, middle.shape, 0) & (S - 1)
    before = jnp.where(column == 0, 0.0, pltpu.roll(middle, 1, 0))
    after = jnp.where(column == S - 1, 0.0, pltpu.roll(middle, wide - 1, 0))
    return before.astype(BF16), middle.astype(BF16), after.astype(BF16)


def grad_kernel(x_ref, c_ref, rows_ref, w_ref, out_ref, xt_ref):
    xt_ref[...] = x_ref[0].astype(F32).T.astype(BF16)
    above, below = rows_ref[2 * S : 3 * S].astype(F32), rows_ref[3 * S : 4 * S].astype(F32)
    grads = jnp.concatenate([above, c_ref[0].astype(F32).T, below], axis=0)
    shifted = jnp.concatenate(beside(grads)[::-1], axis=1)
    act_grad = None
    for i in range(3):
        weight = jnp.concatenate([w_ref[3 * i + j] for j in range(3)], axis=0)
        term = jnp.dot(
            shifted[(2 - i) * S : (2 - i) * S + CELLS], weight, preferred_element_type=F32
        )
        act_grad = term if act_grad is None else act_grad + term
    out_ref[...] = act_grad


def main_kernel(
    mark_ref, xt_ref, cot_ref, rows_ref, in_stat_ref, affine_ref, act_grad_ref,
    strips_ref, in_ref, keep_ref, send_ref, pre_ref, norm_ref, weight_scr,
):
    def mark(k):
        return mark_ref[k : k + 1] > 0.5

    mean, spread = merge([in_stat_ref[k] for k in range(N_NEAR)], LOCAL * N_FAR)
    rstd = lax.rsqrt(spread * (1.0 / ENTRIES) + EPSILON)
    gain, shift = affine_ref[0:1], affine_ref[1:2]
    norm_ref[...] = jnp.concatenate([mean, rstd], axis=0)

    def affine(raw):
        normed = (raw.astype(F32) - mean) * rstd
        pre = normed * gain + shift
        return normed, pre, 1.0 / (1.0 + jnp.exp(-pre))

    def activated(raw):
        _, pre, sig = affine(raw)
        return (pre * sig).astype(BF16).astype(F32)

    top = jnp.where(mark(FIRST), 0.0, activated(rows_ref[0:S]))
    bottom = jnp.where(mark(LAST), 0.0, activated(rows_ref[S : 2 * S]))
    normed, pre, sig = affine(xt_ref[...])
    own = (pre * sig).astype(BF16).astype(F32)
    windows = jnp.concatenate(beside(jnp.concatenate([top, own, bottom], axis=0)), axis=1)
    grad_out = cot_ref[0]
    for i in range(3):
        part = jnp.dot(grad_out, windows[i * S : i * S + CELLS], preferred_element_type=F32)
        for j in range(3):
            weight_scr[3 * i + j] = part[:, j * C : (j + 1) * C]

    halo = activated(turned(in_ref[0:S], mark(BACK))).astype(BF16)
    halo = jnp.concatenate([halo, halo], axis=0)
    strip = strips_ref[S : 2 * S].astype(F32)
    row = lax.broadcasted_iota(jnp.int32, (S, C), 0)
    first, last = row == 0, row == S - 1
    lines = (
        (jnp.where(last, 0.0, pltpu.roll(strip, S - 1, 0)), jnp.where(first & mark(AT_START), strip, 0.0)),
        (strip, jnp.zeros((S, C), F32)),
        (jnp.where(first, 0.0, pltpu.roll(strip, 1, 0)), jnp.where(last & mark(AT_END), strip, 0.0)),
    )
    terms = [
        lax.dot_general(
            jnp.concatenate(pair, axis=0).astype(BF16),
            halo,
            (((0,), (0,)), ((), ())),
            preferred_element_type=F32,
        )
        for pair in lines
    ]
    for e, taps in enumerate(TAPS):
        for tap, term in zip(taps, terms):
            weight_scr[tap] += jnp.where(mark(SIDE + e), term, 0.0)
    second = mark(CORE)

    def put(row, low, high):
        at = pl.ds(row, N_FAR, stride=CHUNK)
        keep_ref[at, :] = jnp.where(second, high, low)
        send_ref[at, :] = jnp.where(second, low, high)

    for tap in range(9):
        for h in range(2):
            put(
                h * 9 + tap,
                weight_scr[tap, h * 64 : h * 64 + 32],
                weight_scr[tap, h * 64 + 32 : (h + 1) * 64],
            )

    pre_grad = act_grad_ref[...] * (sig * (1.0 + pre * (1.0 - sig)))
    pre_ref[...] = pre_grad
    gain_row = jnp.sum(pre_grad * normed, axis=0, keepdims=True)
    shift_row = jnp.sum(pre_grad, axis=0, keepdims=True)
    normed, pre, sig = affine(strips_ref[0:S])
    more = in_ref[S : 2 * S].astype(F32) * (sig * (1.0 + pre * (1.0 - sig)))
    gain_row = gain_row + jnp.sum(more * normed, axis=0, keepdims=True)
    shift_row = shift_row + jnp.sum(more, axis=0, keepdims=True)
    for k, row in ((18, gain_row), (19, shift_row)):
        row = jnp.broadcast_to(row, (N_FAR, C))
        put(k, row, row)


def slope_kernel(xt_ref, norm_ref, affine_ref, out_ref):
    normed = (xt_ref[...].astype(F32) - norm_ref[0:1]) * norm_ref[1:2]
    pre = normed * affine_ref[0:1] + affine_ref[1:2]
    sig = 1.0 / (1.0 + jnp.exp(-pre))
    out_ref[...] = sig * (1.0 + pre * (1.0 - sig))


def end_kernel(
    info_ref, pre_ref, xt_ref, norm_ref, affine_ref, total_ref, in_ref, slope_ref,
    out_ref, gain_sum_ref, shift_sum_ref, side_scr, more_scr,
):
    place = info_ref[0]
    odd = place % 2
    for half in range(2):
        for k in range(2):
            side_scr[2 * half + (odd + k) % 2] = in_ref[half, k]

    def returned(e, start, size):
        at = pl.ds(pl.multiple_of(start, ROWS), size)
        return side_scr[info_ref[1 + e] % 4, at, :].astype(F32)

    more_scr[...] = jnp.zeros((CELLS, C), F32)
    more_scr[0:S] = jnp.where(place == 0, returned(0, 0, S), 0.0)
    more_scr[CELLS - S : CELLS] = jnp.where(place == 3, returned(2, 0, S), 0.0)
    for e, column in ((3, 0), (1, S - 1)):
        more_scr[pl.ds(column, ROWS, stride=S), :] += returned(e, place * ROWS, ROWS)
    mean, rstd = norm_ref[0:1], norm_ref[1:2]
    gain = affine_ref[0:1]
    gain_total, shift_total = total_ref[0:1], total_ref[1:2]
    first = group_sum(gain * shift_total) * (1.0 / ENTRIES)
    second = group_sum(gain * gain_total) * (1.0 / ENTRIES)
    normed = (xt_ref[...].astype(F32) - mean) * rstd
    pre_grad = pre_ref[...] + more_scr[...] * slope_ref[...]
    out = rstd * (pre_grad * gain - first - normed * second)
    out_ref[0] = out.T.astype(BF16)
    gain_sum_ref[...] = gain_total * SCALE
    shift_sum_ref[...] = shift_total * SCALE


def weight_kernel(whole_ref, out_ref):
    for tap in range(9):
        for h in range(2):
            out_ref[tap, h * 64 : (h + 1) * 64] = (
                whole_ref[pl.ds(h * 9 + tap, 64, stride=TAPPED), :] * SCALE
            )


def sum_kernel(parts, copies, in_ref, out_ref):
    rows = in_ref.shape[0] // parts
    total = in_ref[0:rows]
    for k in range(1, parts):
        total = total + in_ref[k * rows : (k + 1) * rows]
    for k in range(copies):
        out_ref[k * rows : (k + 1) * rows] = total


def last_sum_kernel(in_ref, out_ref, sums_ref):
    total = in_ref[0:CHUNK]
    for k in range(1, 8):
        total = total + in_ref[k * CHUNK : (k + 1) * CHUNK]
    for k in range(N_FAR):
        out_ref[k * TAPPED : (k + 1) * TAPPED] = total[0:TAPPED]
    sums_ref[...] = total[TAPPED:CHUNK]


def add_kernel(mark_ref, own_ref, both_ref, out_ref):
    second = mark_ref[CORE : CORE + 1] > 0.5
    out_ref[...] = own_ref[...] + jnp.where(second, both_ref[0], both_ref[1])


def sum_and_pair_kernel(parts, copies, in_ref, own_ref, other_ref, _, out_ref, pair_ref):
    pair_ref[0] = own_ref[S : 2 * S]
    pair_ref[1] = other_ref[S : 2 * S]
    sum_kernel(parts, copies, in_ref, out_ref)


def exchanged(x, axes, parts):
    x = x.reshape(parts, x.shape[0] // parts // 4, 4, C)
    return lax.all_to_all(x, axes, 0, 0, tiled=True)


def shape(dims, dtype):
    return jax.ShapeDtypeStruct(dims, dtype)


def body(features, cotangent, conv_weight, norm_gain, norm_shift, seam_code, corner_map):
    place = lax.axis_index(SUB).astype(jnp.int32).reshape(1)
    core = lax.axis_index("co").astype(jnp.int32).reshape(1)
    info = jnp.concatenate([place, seam_code[0], corner_map[0], core])
    weight = conv_weight.transpose(1, 0, 2)
    gain, shift = norm_gain.reshape(1, C), norm_shift.reshape(1, C)
    edges, stats = pl.pallas_call(
        start_kernel,
        out_shape=(shape((2, EDGE, C), BF16), shape((N_FAR, 1, C), F32)),
        in_specs=[pl.BlockSpec(memory_space=pltpu.HBM)] * 2,
        out_specs=(VMEM,) * 2,
        scratch_shapes=[pltpu.VMEM((C, CELLS), BF16)] * 2 + [pltpu.SemaphoreType.DMA((2, 4))],
        compiler_params=pltpu.CompilerParams(vmem_limit_bytes=START_VMEM),
    )(features, cotangent)
    came = lax.ppermute(edges, "z2", [(0, 1), (1, 0)])
    stats = lax.all_to_all(stats, FAR, 0, 0, tiled=True)
    send, keep, affine, marks = pl.pallas_call(
        middle_kernel,
        out_shape=(
            shape((3, LINE, C), BF16),
            shape((LINE, C), BF16),
            shape((2, C), F32),
            shape((16, C), F32),
        ),
        in_specs=[SMEM] + [VMEM] * 4,
        out_specs=(VMEM,) * 4,
        scratch_shapes=[pltpu.VMEM((2, 4, S, C), BF16)],
        compiler_params=PARAMS,
    )(info, edges, came, gain, shift)
    came = lax.all_gather(send, "z1", axis=0, tiled=False)
    message, strips, rows, stats = pl.pallas_call(
        seam_kernel,
        out_shape=(
            shape((LINE, C), BF16),
            shape((LINE, C), BF16),
            shape((2 * LINE, C), BF16),
            shape((N_NEAR, 1, C), F32),
        ),
        in_specs=[VMEM] * 5,
        out_specs=(VMEM,) * 4,
        compiler_params=PARAMS,
    )(marks, keep, came, stats, weight)
    message = lax.ppermute(
        message,
        tuple(AXES),
        [(4 * t + s, 4 * ((t + STEPS[s]) % 128) + (s + 2) % 4) for t in range(128) for s in range(4)],
    )
    stats = lax.all_to_all(stats, NEAR, 0, 0, tiled=True)
    act_grad, xt = pl.pallas_call(
        grad_kernel,
        out_shape=(shape((CELLS, C), F32), shape((CELLS, C), BF16)),
        in_specs=[VMEM] * 4,
        out_specs=(VMEM,) * 2,
        compiler_params=PARAMS,
        cost_estimate=pl.CostEstimate(
            flops=18 * CELLS * C * C, bytes_accessed=10 * CELLS * C, transcendentals=0
        ),
    )(features, cotangent, rows, weight)
    parts, send, pre_grad, norm = pl.pallas_call(
        main_kernel,
        out_shape=(
            shape((N_FAR * CHUNK, C), F32),
            shape((N_FAR * CHUNK, C), F32),
            shape((CELLS, C), F32),
            shape((2, C), F32),
        ),
        in_specs=[VMEM] * 9,
        out_specs=(VMEM,) * 4,
        scratch_shapes=[pltpu.VMEM((9, C, C), F32)],
        compiler_params=PARAMS,
    )(marks, xt, cotangent, rows, stats, affine, act_grad, strips, message)
    slope = pl.pallas_call(
        slope_kernel,
        out_shape=shape((CELLS, C), F32),
        in_specs=[VMEM] * 3,
        out_specs=VMEM,
        compiler_params=PARAMS,
    )(xt, norm, affine)
    other = lax.ppermute(message, "z1", [(0, 1), (1, 0)])
    both = lax.all_gather(send, "co", axis=0, tiled=False)
    parts = pl.pallas_call(
        add_kernel,
        out_shape=shape((N_FAR * CHUNK, C), F32),
        in_specs=[VMEM] * 3,
        out_specs=VMEM,
        compiler_params=PARAMS,
    )(marks, parts, both)
    parts, pair = pl.pallas_call(
        functools.partial(sum_and_pair_kernel, N_FAR, 8),
        out_shape=(shape((8 * CHUNK, C), F32), shape((2, S, C), BF16)),
        in_specs=[VMEM] * 4,
        out_specs=(VMEM,) * 2,
        compiler_params=PARAMS,
    )(exchanged(parts, FAR, N_FAR).reshape(N_FAR * CHUNK, C), message, other, slope)
    sides = lax.all_gather(pair, "z2", axis=0, tiled=False)
    parts, sums = pl.pallas_call(
        last_sum_kernel,
        out_shape=(shape((N_FAR * TAPPED, C), F32), shape((2, C), F32)),
        in_specs=[VMEM],
        out_specs=(VMEM,) * 2,
        compiler_params=PARAMS,
    )(exchanged(parts, ("zh", "z2", "z1"), 8).reshape(8 * CHUNK, C))
    half = lax.all_to_all(parts.reshape(N_FAR, TAPPED // 2, 2, C), FAR, 0, 0, tiled=True)
    whole = lax.all_gather(half, "co", axis=0, tiled=True)
    grad_input, grad_gain, grad_shift = pl.pallas_call(
        end_kernel,
        out_shape=(shape((1, C, CELLS), BF16), shape((1, C), F32), shape((1, C), F32)),
        in_specs=[SMEM] + [VMEM] * 7,
        out_specs=(VMEM,) * 3,
        scratch_shapes=[pltpu.VMEM((4, S, C), BF16), pltpu.VMEM((CELLS, C), F32)],
        compiler_params=PARAMS,
    )(info, pre_grad, xt, norm, affine, sums, sides, slope)
    grad_weight = pl.pallas_call(
        weight_kernel,
        out_shape=shape((9, C, C), F32),
        in_specs=[VMEM],
        out_specs=VMEM,
        compiler_params=PARAMS,
    )(whole.reshape(64 * TAPPED, C)).transpose(1, 0, 2)
    return grad_input, grad_weight, grad_gain.reshape(C), grad_shift.reshape(C)


def solution(mesh):
    fine = Mesh(mesh.devices.reshape(tuple(AXES.values())), tuple(AXES))
    return jax.shard_map(
        body,
        mesh=fine,
        in_specs=(
            P(TILE, None, SUB),
            P(TILE, None, SUB),
            P(),
            P(),
            P(),
            P(TILE, None),
            P(TILE, None),
        ),
        out_specs=(P(TILE, None, SUB), P(), P(), P()),
        check_vma=False,
    )
```

```python
import functools
import math

import jax
import jax.numpy as jnp
from jax import lax
from jax.experimental import pallas as pl
from jax.experimental.pallas import tpu as pltpu
from jax.sharding import Mesh
from jax.sharding import PartitionSpec as P

GC = 4
S = 64
PER_GROUP = 8
EPSILON = 1e-05
STEPS = (-GC, 1, GC, -1)
ROWS = 16
CELLS = ROWS * S
C = 128
LINE = 2 * S
EDGE = 2 * S + 2 * ROWS
CHUNK = 20
TAPPED = 18

TILE = ("y", "x", "zh", "co")
AXES = {"y": 8, "x": 4, "zh": 2, "co": 2, "z2": 2, "z1": 2}
SUB = ("z2", "z1")
NEAR = ("zh", "co", "z2", "z1")
FAR = ("y", "x")
N_NEAR = 16
N_FAR = 32
DEVICES = 512
ENTRIES = DEVICES * CELLS * PER_GROUP
LOCAL = CELLS * PER_GROUP
SCALE = 1.0 / math.sqrt(DEVICES * CELLS)

F32 = jnp.float32
BF16 = jnp.bfloat16
VMEM = pl.BlockSpec(memory_space=pltpu.VMEM)
SMEM = pl.BlockSpec(memory_space=pltpu.SMEM)
START_VMEM = 56360960
PARAMS = pltpu.CompilerParams(vmem_limit_bytes=40 * 1024 * 1024)


def group_sum(row):
    total = jnp.broadcast_to(row, (8, C))
    lane = lax.broadcasted_iota(jnp.int32, (8, C), 1)
    for by in (1, 2, 4):
        other = jnp.where(
            (lane & by) != 0, pltpu.roll(total, by, 1), pltpu.roll(total, C - by, 1)
        )
        total = total + other
    return total[0:1]


def packed(mean, spread):
    lane = lax.broadcasted_iota(jnp.int32, (1, C), 1)
    return jnp.where(lane % 2 == 0, mean, spread)


def unpacked(row):
    row = jnp.broadcast_to(row, (8, C))
    even = lax.broadcasted_iota(jnp.int32, (8, C), 1) % 2 == 0
    mean = jnp.where(even, row, pltpu.roll(row, 1, 1))
    spread = jnp.where(even, pltpu.roll(row, C - 1, 1), row)
    return mean[0:1], spread[0:1]


def merge(rows, count):
    means, squares = zip(*[unpacked(row) for row in rows])
    mean = sum(means) * (1.0 / len(means))
    spread = sum(squares) + float(count) * sum((m - mean) * (m - mean) for m in means)
    return mean, spread


def edge_picker():
    row = lax.broadcasted_iota(jnp.int32, (EDGE, CELLS), 0)
    cell = lax.broadcasted_iota(jnp.int32, (EDGE, CELLS), 1)
    wanted = jnp.where(row < S, row, row + CELLS - 2 * S)
    wanted = jnp.where(row >= 2 * S, (row - 2 * S) * S + S - 1, wanted)
    wanted = jnp.where(row >= 2 * S + ROWS, (row - 2 * S - ROWS) * S, wanted)
    return jnp.where(cell == wanted, 1.0, 0.0).astype(BF16)


def start_kernel(x_hbm, c_hbm, edge_ref, stat_ref, x_in, c_in, sems):
    copies = []
    for kind, (far, near) in enumerate(((x_hbm, x_in), (c_hbm, c_in))):
        for k in range(4):
            at = pl.ds(k * 32, 32)
            copies.append(pltpu.make_async_copy(far.at[0, at], near.at[at], sems.at[kind, k]))
            copies[-1].start()
    picker = edge_picker()
    for copy in copies[:4]:
        copy.wait()
    x = x_in[...].astype(F32)
    blocks = [x[:, k * C : (k + 1) * C] for k in range(CELLS // C)]

    def channel_sums(parts):
        return group_sum(jnp.sum(sum(parts).T, axis=0, keepdims=True))

    mean = channel_sums(blocks) * (1.0 / LOCAL)
    column = jnp.broadcast_to(mean, (C, C)).T
    spread = channel_sums([(v - column) * (v - column) for v in blocks])
    stat_ref[...] = jnp.broadcast_to(packed(mean, spread)[None], (N_FAR, 1, C))
    for copy in copies[4:]:
        copy.wait()
    for kind, ref in enumerate((x_in, c_in)):
        edge_ref[kind] = lax.dot_general(
            picker, ref[...], (((1,), (1,)), ((), ())), preferred_element_type=F32
        ).astype(BF16)


def corners_of(info_ref, side):
    start = jnp.where(side == 1, 1, jnp.where(side == 2, 3, 0))
    end = jnp.where(side == 0, 1, jnp.where(side == 3, 3, 2))
    return info_ref[5 + start] == side % 2, info_ref[5 + end] == side % 2


TAPS = ((0, 1, 2), (2, 5, 8), (6, 7, 8), (0, 3, 6))
FIRST, LAST, CORE, SIDE, AT_START, AT_END, BACK, ODD = 0, 1, 2, 3, 7, 8, 9, 10


def middle_kernel(
    info_ref, own_ref, other_ref, gain_ref, shift_ref,
    send_ref, left_ref, affine_ref, mark_ref, side_scr,
):
    place = info_ref[0]
    odd = place % 2
    pair = (place + 2) % 4
    affine_ref[0:1], affine_ref[1:2] = gain_ref[...], shift_ref[...]
    mine = side_facing(info_ref, place)
    at_start, at_end = corners_of(info_ref, mine)
    marks = (
        [place == 0, place == 3, info_ref[9] == 1]
        + [mine == e for e in range(4)]
        + [at_start, at_end, info_ref[1 + mine] // 4 == 1, odd == 1]
    )
    for k, mark in enumerate(marks):
        mark_ref[k : k + 1] = jnp.full((1, C), jnp.where(mark, 1.0, 0.0), F32)
    zero = jnp.zeros((S, C), BF16)
    first, last = slice(0, S), slice(S, 2 * S)
    for kind in range(2):
        side_scr[kind, 0] = jnp.where(
            place == 0, own_ref[kind, first], jnp.where(pair == 0, other_ref[kind, first], zero)
        )
        side_scr[kind, 2] = jnp.where(
            place == 3, own_ref[kind, last], jnp.where(pair == 3, other_ref[kind, last], zero)
        )
        for k, side in enumerate((1, 3)):
            at = slice(2 * S + k * ROWS, 2 * S + (k + 1) * ROWS)
            side_scr[kind, side] = zero
            for who, ref in ((place, own_ref), (pair, other_ref)):
                rows = pl.ds(pl.multiple_of(who * ROWS, ROWS), ROWS)
                side_scr[kind, side, rows, :] = ref[kind, at]
        here = slice(kind * S, (kind + 1) * S)
        send_ref[0, here] = side_scr[kind, side_facing(info_ref, place + 1 - 2 * odd)]
        left_ref[here] = side_scr[kind, side_facing(info_ref, place)]
        send_ref[1, here] = jnp.where(odd == 1, own_ref[kind, first], own_ref[kind, last])
        send_ref[2, here] = jnp.where(place == 0, other_ref[kind, first], other_ref[kind, last])


def side_facing(info_ref, direction):
    side = jnp.int32(0)
    for e in range(1, 4):
        side = jnp.where(info_ref[1 + e] % 4 == direction, e, side)
    return side


def flip_matrix():
    a = lax.broadcasted_iota(jnp.int32, (S, S), 0)
    b = lax.broadcasted_iota(jnp.int32, (S, S), 1)
    return jnp.where(a + b == S - 1, 1.0, 0.0).astype(BF16)


def turned(strip, flag):
    back = jnp.dot(flip_matrix(), strip, preferred_element_type=F32)
    return jnp.where(flag, back, strip.astype(F32)).astype(BF16)


def seam_kernel(
    mark_ref, keep_ref, in_ref, in_stat_ref, w_ref, message_ref, strips_ref, rows_ref, stat_ref,
):
    def mark(k):
        return mark_ref[k : k + 1] > 0.5

    def other(k):
        return jnp.where(mark(ODD), in_ref[0, k].astype(F32), in_ref[1, k].astype(F32))

    strips = (keep_ref[...].astype(F32) + other(0)).astype(BF16)
    strips_ref[...] = strips
    grads = strips[S : 2 * S]
    parts = []
    for k in range(3):
        weight = w_ref[TAPS[0][k]].astype(F32)
        for e in range(1, 4):
            weight = jnp.where(mark(SIDE + e), w_ref[TAPS[e][k]].astype(F32), weight)
        parts.append(jnp.dot(grads, weight.astype(BF16), preferred_element_type=F32))
    row = lax.broadcasted_iota(jnp.int32, (S, C), 0)
    first, last = row == 0, row == S - 1
    grad = parts[1]
    grad = grad + jnp.where(last, 0.0, pltpu.roll(parts[0], S - 1, 0))
    grad = grad + jnp.where(first, 0.0, pltpu.roll(parts[2], 1, 0))
    grad = grad + jnp.where(first & mark(AT_START), parts[0], 0.0)
    grad = grad + jnp.where(last & mark(AT_END), parts[2], 0.0)
    message_ref[0:S] = strips[0:S]
    message_ref[S : 2 * S] = turned(grad.astype(BF16), mark(BACK))
    direct, passed = other(1), other(2)
    above = jnp.where(mark(ODD), direct, passed)
    below = jnp.where(mark(ODD), passed, direct)
    rows_ref[0:S] = above[0:S].astype(BF16)
    rows_ref[S : 2 * S] = below[0:S].astype(BF16)
    rows_ref[2 * S : 3 * S] = jnp.where(mark(FIRST), 0.0, above[S : 2 * S]).astype(BF16)
    rows_ref[3 * S : 4 * S] = jnp.where(mark(LAST), 0.0, below[S : 2 * S]).astype(BF16)
    stats = packed(*merge([in_stat_ref[k] for k in range(N_FAR)], LOCAL))
    stat_ref[...] = jnp.broadcast_to(stats[None], (N_NEAR, 1, C))


def beside(middle):
    wide = middle.shape[0]
    column = lax.broadcasted_iota(jnp.int32, middle.shape, 0) & (S - 1)
    before = jnp.where(column == 0, 0.0, pltpu.roll(middle, 1, 0))
    after = jnp.where(column == S - 1, 0.0, pltpu.roll(middle, wide - 1, 0))
    return before.astype(BF16), middle.astype(BF16), after.astype(BF16)


def grad_kernel(x_ref, c_ref, rows_ref, w_ref, out_ref, xt_ref):
    xt_ref[...] = x_ref[0].astype(F32).T.astype(BF16)
    above, below = rows_ref[2 * S : 3 * S].astype(F32), rows_ref[3 * S : 4 * S].astype(F32)
    grads = jnp.concatenate([above, c_ref[0].astype(F32).T, below], axis=0)
    shifted = jnp.concatenate(beside(grads)[::-1], axis=1)
    act_grad = None
    for i in range(3):
        weight = jnp.concatenate([w_ref[3 * i + j] for j in range(3)], axis=0)
        term = jnp.dot(
            shifted[(2 - i) * S : (2 - i) * S + CELLS], weight, preferred_element_type=F32
        )
        act_grad = term if act_grad is None else act_grad + term
    out_ref[...] = act_grad


def main_kernel(
    mark_ref, xt_ref, cot_ref, rows_ref, in_stat_ref, affine_ref, act_grad_ref,
    strips_ref, in_ref, keep_ref, send_ref, pre_ref, norm_ref, weight_scr,
):
    def mark(k):
        return mark_ref[k : k + 1] > 0.5

    mean, spread = merge([in_stat_ref[k] for k in range(N_NEAR)], LOCAL * N_FAR)
    rstd = lax.rsqrt(spread * (1.0 / ENTRIES) + EPSILON)
    gain, shift = affine_ref[0:1], affine_ref[1:2]
    norm_ref[...] = jnp.concatenate([mean, rstd], axis=0)

    def affine(raw):
        normed = (raw.astype(F32) - mean) * rstd
        pre = normed * gain + shift
        return normed, pre, 1.0 / (1.0 + jnp.exp(-pre))

    def activated(raw):
        _, pre, sig = affine(raw)
        return (pre * sig).astype(BF16).astype(F32)

    top = jnp.where(mark(FIRST), 0.0, activated(rows_ref[0:S]))
    bottom = jnp.where(mark(LAST), 0.0, activated(rows_ref[S : 2 * S]))
    normed, pre, sig = affine(xt_ref[...])
    own = (pre * sig).astype(BF16).astype(F32)
    windows = jnp.concatenate(beside(jnp.concatenate([top, own, bottom], axis=0)), axis=1)
    grad_out = cot_ref[0]
    for i in range(3):
        part = jnp.dot(grad_out, windows[i * S : i * S + CELLS], preferred_element_type=F32)
        for j in range(3):
            weight_scr[3 * i + j] = part[:, j * C : (j + 1) * C]

    halo = activated(turned(in_ref[0:S], mark(BACK))).astype(BF16)
    halo = jnp.concatenate([halo, halo], axis=0)
    strip = strips_ref[S : 2 * S].astype(F32)
    row = lax.broadcasted_iota(jnp.int32, (S, C), 0)
    first, last = row == 0, row == S - 1
    lines = (
        (jnp.where(last, 0.0, pltpu.roll(strip, S - 1, 0)), jnp.where(first & mark(AT_START), strip, 0.0)),
        (strip, jnp.zeros((S, C), F32)),
        (jnp.where(first, 0.0, pltpu.roll(strip, 1, 0)), jnp.where(last & mark(AT_END), strip, 0.0)),
    )
    terms = [
        lax.dot_general(
            jnp.concatenate(pair, axis=0).astype(BF16),
            halo,
            (((0,), (0,)), ((), ())),
            preferred_element_type=F32,
        )
        for pair in lines
    ]
    for e, taps in enumerate(TAPS):
        for tap, term in zip(taps, terms):
            weight_scr[tap] += jnp.where(mark(SIDE + e), term, 0.0)
    second = mark(CORE)

    def put(row, low, high):
        at = pl.ds(row, N_FAR, stride=CHUNK)
        keep_ref[at, :] = jnp.where(second, high, low)
        send_ref[at, :] = jnp.where(second, low, high)

    for tap in range(9):
        for h in range(2):
            put(
                h * 9 + tap,
                weight_scr[tap, h * 64 : h * 64 + 32],
                weight_scr[tap, h * 64 + 32 : (h + 1) * 64],
            )

    pre_grad = act_grad_ref[...] * (sig * (1.0 + pre * (1.0 - sig)))
    pre_ref[...] = pre_grad
    gain_row = jnp.sum(pre_grad * normed, axis=0, keepdims=True)
    shift_row = jnp.sum(pre_grad, axis=0, keepdims=True)
    normed, pre, sig = affine(strips_ref[0:S])
    more = in_ref[S : 2 * S].astype(F32) * (sig * (1.0 + pre * (1.0 - sig)))
    gain_row = gain_row + jnp.sum(more * normed, axis=0, keepdims=True)
    shift_row = shift_row + jnp.sum(more, axis=0, keepdims=True)
    for k, row in ((18, gain_row), (19, shift_row)):
        row = jnp.broadcast_to(row, (N_FAR, C))
        put(k, row, row)


def slope_kernel(xt_ref, norm_ref, affine_ref, out_ref):
    normed = (xt_ref[...].astype(F32) - norm_ref[0:1]) * norm_ref[1:2]
    pre = normed * affine_ref[0:1] + affine_ref[1:2]
    sig = 1.0 / (1.0 + jnp.exp(-pre))
    out_ref[...] = sig * (1.0 + pre * (1.0 - sig))


def end_kernel(
    info_ref, pre_ref, xt_ref, norm_ref, affine_ref, total_ref, in_ref, slope_ref,
    out_ref, gain_sum_ref, shift_sum_ref, side_scr, more_scr,
):
    place = info_ref[0]
    odd = place % 2
    for half in range(2):
        for k in range(2):
            side_scr[2 * half + (odd + k) % 2] = in_ref[half, k]

    def returned(e, start, size):
        at = pl.ds(pl.multiple_of(start, ROWS), size)
        return side_scr[info_ref[1 + e] % 4, at, :].astype(F32)

    more_scr[...] = jnp.zeros((CELLS, C), F32)
    more_scr[0:S] = jnp.where(place == 0, returned(0, 0, S), 0.0)
    more_scr[CELLS - S : CELLS] = jnp.where(place == 3, returned(2, 0, S), 0.0)
    for e, column in ((3, 0), (1, S - 1)):
        more_scr[pl.ds(column, ROWS, stride=S), :] += returned(e, place * ROWS, ROWS)
    mean, rstd = norm_ref[0:1], norm_ref[1:2]
    gain = affine_ref[0:1]
    gain_total, shift_total = total_ref[0:1], total_ref[1:2]
    first = group_sum(gain * shift_total) * (1.0 / ENTRIES)
    second = group_sum(gain * gain_total) * (1.0 / ENTRIES)
    normed = (xt_ref[...].astype(F32) - mean) * rstd
    pre_grad = pre_ref[...] + more_scr[...] * slope_ref[...]
    out = rstd * (pre_grad * gain - first - normed * second)
    out_ref[0] = out.T.astype(BF16)
    gain_sum_ref[...] = gain_total * SCALE
    shift_sum_ref[...] = shift_total * SCALE


def weight_kernel(whole_ref, out_ref):
    for tap in range(9):
        for h in range(2):
            out_ref[tap, h * 64 : (h + 1) * 64] = (
                whole_ref[pl.ds(h * 9 + tap, 64, stride=TAPPED), :] * SCALE
            )


def sum_kernel(parts, copies, in_ref, out_ref):
    rows = in_ref.shape[0] // parts
    total = in_ref[0:rows]
    for k in range(1, parts):
        total = total + in_ref[k * rows : (k + 1) * rows]
    for k in range(copies):
        out_ref[k * rows : (k + 1) * rows] = total


def last_sum_kernel(in_ref, out_ref, sums_ref):
    total = in_ref[0:CHUNK]
    for k in range(1, 8):
        total = total + in_ref[k * CHUNK : (k + 1) * CHUNK]
    for k in range(N_FAR):
        out_ref[k * TAPPED : (k + 1) * TAPPED] = total[0:TAPPED]
    sums_ref[...] = total[TAPPED:CHUNK]


def add_kernel(mark_ref, own_ref, both_ref, out_ref):
    second = mark_ref[CORE : CORE + 1] > 0.5
    out_ref[...] = own_ref[...] + jnp.where(second, both_ref[0], both_ref[1])


def sum_and_pair_kernel(parts, copies, in_ref, own_ref, other_ref, _, out_ref, pair_ref):
    pair_ref[0] = own_ref[S : 2 * S]
    pair_ref[1] = other_ref[S : 2 * S]
    sum_kernel(parts, copies, in_ref, out_ref)


def exchanged(x, axes, parts):
    x = x.reshape(parts, x.shape[0] // parts // 2, 2, C)
    return lax.all_to_all(x, axes, 0, 0, tiled=True)


def shape(dims, dtype):
    return jax.ShapeDtypeStruct(dims, dtype)


def body(features, cotangent, conv_weight, norm_gain, norm_shift, seam_code, corner_map):
    place = lax.axis_index(SUB).astype(jnp.int32).reshape(1)
    core = lax.axis_index("co").astype(jnp.int32).reshape(1)
    info = jnp.concatenate([place, seam_code[0], corner_map[0], core])
    weight = conv_weight.transpose(1, 0, 2)
    gain, shift = norm_gain.reshape(1, C), norm_shift.reshape(1, C)
    edges, stats = pl.pallas_call(
        start_kernel,
        out_shape=(shape((2, EDGE, C), BF16), shape((N_FAR, 1, C), F32)),
        in_specs=[pl.BlockSpec(memory_space=pltpu.HBM)] * 2,
        out_specs=(VMEM,) * 2,
        scratch_shapes=[pltpu.VMEM((C, CELLS), BF16)] * 2 + [pltpu.SemaphoreType.DMA((2, 4))],
        compiler_params=pltpu.CompilerParams(vmem_limit_bytes=START_VMEM),
    )(features, cotangent)
    came = lax.ppermute(edges, "z2", [(0, 1), (1, 0)])
    stats = lax.all_to_all(stats, FAR, 0, 0, tiled=True)
    send, keep, affine, marks = pl.pallas_call(
        middle_kernel,
        out_shape=(
            shape((3, LINE, C), BF16),
            shape((LINE, C), BF16),
            shape((2, C), F32),
            shape((16, C), F32),
        ),
        in_specs=[SMEM] + [VMEM] * 4,
        out_specs=(VMEM,) * 4,
        scratch_shapes=[pltpu.VMEM((2, 4, S, C), BF16)],
        compiler_params=PARAMS,
    )(info, edges, came, gain, shift)
    came = lax.all_gather(send, "z1", axis=0, tiled=False)
    message, strips, rows, stats = pl.pallas_call(
        seam_kernel,
        out_shape=(
            shape((LINE, C), BF16),
            shape((LINE, C), BF16),
            shape((2 * LINE, C), BF16),
            shape((N_NEAR, 1, C), F32),
        ),
        in_specs=[VMEM] * 5,
        out_specs=(VMEM,) * 4,
        compiler_params=PARAMS,
    )(marks, keep, came, stats, weight)
    message = lax.ppermute(
        message,
        tuple(AXES),
        [(4 * t + s, 4 * ((t + STEPS[s]) % 128) + (s + 2) % 4) for t in range(128) for s in range(4)],
    )
    stats = lax.all_to_all(stats, NEAR, 0, 0, tiled=True)
    act_grad, xt = pl.pallas_call(
        grad_kernel,
        out_shape=(shape((CELLS, C), F32), shape((CELLS, C), BF16)),
        in_specs=[VMEM] * 4,
        out_specs=(VMEM,) * 2,
        compiler_params=PARAMS,
        cost_estimate=pl.CostEstimate(
            flops=18 * CELLS * C * C, bytes_accessed=10 * CELLS * C, transcendentals=0
        ),
    )(features, cotangent, rows, weight)
    parts, send, pre_grad, norm = pl.pallas_call(
        main_kernel,
        out_shape=(
            shape((N_FAR * CHUNK, C), F32),
            shape((N_FAR * CHUNK, C), F32),
            shape((CELLS, C), F32),
            shape((2, C), F32),
        ),
        in_specs=[VMEM] * 9,
        out_specs=(VMEM,) * 4,
        scratch_shapes=[pltpu.VMEM((9, C, C), F32)],
        compiler_params=PARAMS,
    )(marks, xt, cotangent, rows, stats, affine, act_grad, strips, message)
    slope = pl.pallas_call(
        slope_kernel,
        out_shape=shape((CELLS, C), F32),
        in_specs=[VMEM] * 3,
        out_specs=VMEM,
        compiler_params=PARAMS,
    )(xt, norm, affine)
    other = lax.ppermute(message, "z1", [(0, 1), (1, 0)])
    both = lax.all_gather(send, "co", axis=0, tiled=False)
    parts = pl.pallas_call(
        add_kernel,
        out_shape=shape((N_FAR * CHUNK, C), F32),
        in_specs=[VMEM] * 3,
        out_specs=VMEM,
        compiler_params=PARAMS,
    )(marks, parts, both)
    parts, pair = pl.pallas_call(
        functools.partial(sum_and_pair_kernel, N_FAR, 8),
        out_shape=(shape((8 * CHUNK, C), F32), shape((2, S, C), BF16)),
        in_specs=[VMEM] * 4,
        out_specs=(VMEM,) * 2,
        compiler_params=PARAMS,
    )(exchanged(parts, FAR, N_FAR).reshape(N_FAR * CHUNK, C), message, other, slope)
    sides = lax.all_gather(pair, "z2", axis=0, tiled=False)
    parts, sums = pl.pallas_call(
        last_sum_kernel,
        out_shape=(shape((N_FAR * TAPPED, C), F32), shape((2, C), F32)),
        in_specs=[VMEM],
        out_specs=(VMEM,) * 2,
        compiler_params=PARAMS,
    )(exchanged(parts, ("zh", "z2", "z1"), 8).reshape(8 * CHUNK, C))
    half = lax.all_to_all(parts.reshape(N_FAR, TAPPED // 2, 2, C), FAR, 0, 0, tiled=True)
    whole = lax.all_gather(half, "co", axis=0, tiled=True)
    grad_input, grad_gain, grad_shift = pl.pallas_call(
        end_kernel,
        out_shape=(shape((1, C, CELLS), BF16), shape((1, C), F32), shape((1, C), F32)),
        in_specs=[SMEM] + [VMEM] * 7,
        out_specs=(VMEM,) * 3,
        scratch_shapes=[pltpu.VMEM((4, S, C), BF16), pltpu.VMEM((CELLS, C), F32)],
        compiler_params=PARAMS,
    )(info, pre_grad, xt, norm, affine, sums, sides, slope)
    grad_weight = pl.pallas_call(
        weight_kernel,
        out_shape=shape((9, C, C), F32),
        in_specs=[VMEM],
        out_specs=VMEM,
        compiler_params=PARAMS,
    )(whole.reshape(64 * TAPPED, C)).transpose(1, 0, 2)
    return grad_input, grad_weight, grad_gain.reshape(C), grad_shift.reshape(C)


def solution(mesh):
    fine = Mesh(mesh.devices.reshape(tuple(AXES.values())), tuple(AXES))
    return jax.shard_map(
        body,
        mesh=fine,
        in_specs=(
            P(TILE, None, SUB),
            P(TILE, None, SUB),
            P(),
            P(),
            P(),
            P(TILE, None),
            P(TILE, None),
        ),
        out_specs=(P(TILE, None, SUB), P(), P(), P()),
        check_vma=False,
    )
```
